256 devices in a mesh: ctx: 32 (over z, y), head: 8 (over x, core).
Axes of the slice: x: 4, y: 4, z: 8, core: 2. Of those that a mesh axis runs over, the one named last changes fastest.
Arguments:
- x_in: bfloat16 [49152, 8192], P('ctx', 'head'), may hold values from -6 to 6
- gate_z: bfloat16 [49152, 8192], P('ctx', 'head'), may hold values from -6 to 6
- bc_in: bfloat16 [49152, 8, 256], P('ctx', 'head'), may hold values from -6 to 6
- dt_raw: float32 [49152, 128], P('ctx', 'head'), may hold values from -4 to 4
- conv_x: float32 [4, 8192], P(None, 'head'), may hold values from -3 to 3
- conv_bc: float32 [4, 8, 256], P(None, 'head'), may hold values from -3 to 3
- dt_bias: float32 [128], P('head'), may hold values from -11 to -1
- a_log: float32 [128], P('head'), may hold values from -3 to 1
- d_skip: float32 [128], P('head'), may hold values from 0.5 to 2
- norm_gain: float32 [8192], P('head'), may hold values from 0.5 to 1.5
- readout: bfloat16 [8192], P('head'), may hold values from -0.0625 to 0.0625
- lengths: int32 [16], replicated, may hold values from 1 to 24576, 49152 in all
Outputs:
- mixed_out: bfloat16 [49152, 8192], P('ctx', 'head')
- cand_scores: float32 [16], replicated
The draws below stay inside these ranges and needn't reach their ends.
Inputs may be any that keep to these rules, and one draw needn't show every extreme that they name: `lengths`: candidate token counts; they sum to 49152, and one candidate has exactly 24576 tokens.
All inputs are finite; a program needn't handle non-finite values.
Results may differ from the reference program's by a relative error of at most 0.009.
Values may be sent and summed in bfloat16 or wider, within the bound.
A program may use at most 128 MiB of HBM per device.

```python
import math
import jax
import jax.numpy as jnp
import numpy as np
from jax import lax

HEADS = 128
STATE = 128
GROUPS = 8
STRETCH = 256
INNER = 8192
TOKENS = 49152
CANDS = 16


def slow_heads(key, share):
    return jax.random.randint(key, (HEADS,), 0, 10) < share


def draw_dt_bias(key, part):
    share = 5
    slow = slow_heads(key, share)
    key = jax.random.fold_in(key, 11)
    jitter = jax.random.uniform(jax.random.fold_in(key, 1), (HEADS,), jnp.float32, -0.5, 0.5)
    fast_value = jax.random.uniform(jax.random.fold_in(key, 2), (HEADS,), jnp.float32, -3.0, -2.0)
    slow_value = jnp.log(jnp.float32(4.0) / jnp.float32(TOKENS)) + jitter
    return jnp.where(slow, slow_value, fast_value).astype(jnp.float32)


def draw_a_log(key, part):
    share = 5
    slow = slow_heads(key, share)
    key = jax.random.fold_in(key, 12)
    slow_value = jax.random.uniform(jax.random.fold_in(key, 1), (HEADS,), jnp.float32, -2.6, -1.2)
    fast_value = jax.random.uniform(jax.random.fold_in(key, 2), (HEADS,), jnp.float32, -1.5, 0.5)
    return jnp.where(slow, slow_value, fast_value).astype(jnp.float32)


def levels(stream_key, extent, split, low, high):
    def one(axis_at, blocks):
        steps = jax.random.uniform(jax.random.fold_in(jax.random.fold_in(stream_key, 6), axis_at), (blocks,), jnp.float32, low / len(split), high / len(split))
        return jnp.repeat(jnp.exp(steps), extent[axis_at] // blocks).reshape((-1,) + (1,) * (len(extent) - axis_at - 1))

    loudness = one(*split[0])
    for cut in split[1:]:
        loudness = loudness * one(*cut)
    return loudness


def length_profile(number_of, total, bound, skew):
    weights = [(1 << 20) // math.isqrt(rank ** skew) + 1 for rank in range(2, number_of + 1)]
    spare, holding = total - bound - (number_of - 1), [1] * (number_of - 1)
    while spare > 0:
        movable = [i for i in range(number_of - 1) if holding[i] < bound]
        mass, left = sum([weights[i] for i in movable]), spare
        for i in movable:
            extra = min(bound - holding[i], max(1, left * weights[i] // mass), spare)
            holding[i] = holding[i] + extra
            spare = spare - extra
    return np.array([bound] + holding)


def uneven_parts(key, number_of, total, limit, lean):
    if number_of == 2:
        one = jax.random.randint(key, (), max(1, total - limit), min(limit, total - 1) + 1)
        return jnp.stack([one, total - one])
    sizes = jnp.asarray(length_profile(number_of, total, limit, lean), jnp.int32)
    pairs = (number_of - 1) // 2
    donor, taker = sizes[1:1 + 2 * pairs:2], sizes[2:2 + 2 * pairs:2]
    room = jnp.minimum(donor - 1, limit - taker)
    passed = jax.random.randint(jax.random.fold_in(key, 1), (pairs,), 0, 1 << 20) % (room + 1)
    sizes = sizes.at[1:1 + 2 * pairs:2].set(donor - passed).at[2:2 + 2 * pairs:2].set(taker + passed)
    return sizes[jax.random.permutation(jax.random.fold_in(key, 2), number_of)]


def normal_values(own_key, dims, spread, reach, shards=(), kind=jnp.bfloat16):
    array = spread * jax.random.normal(own_key, dims, jnp.float32)
    if shards:
        array = array * levels(own_key, dims, shards, -0.22, 0.18)
    return jnp.clip(array, -reach, reach).astype(kind)


def setup_inputs(seed: int = 0) -> dict:
    keys = jax.random.split(jax.random.key(seed), 13)
    x_in = normal_values(keys[0], (TOKENS, INNER), 1.0, 6.0, ((0, 32), (1, 8)))
    gate_z = normal_values(keys[1], (TOKENS, INNER), 1.0, 6.0, ((0, 32), (1, 8)))
    bc_in = normal_values(keys[2], (TOKENS, GROUPS, 2 * STATE), 1.0, 6.0, ((0, 32), (1, 8)))
    dt_raw = normal_values(keys[3], (TOKENS, HEADS), 1.0, 4.0, ((0, 32), (1, 8)), jnp.float32)
    conv_x = normal_values(keys[4], (4, INNER), 4 ** -0.5, 3.0, ((1, 8),), jnp.float32)
    conv_bc = normal_values(keys[5], (4, GROUPS, 2 * STATE), 4 ** -0.5, 3.0, ((1, 8),), jnp.float32)
    dt_bias = draw_dt_bias(jax.random.fold_in(keys[12], 71), 0)
    a_log = draw_a_log(jax.random.fold_in(keys[12], 71), 0)
    d_skip = jnp.clip(0.5 + 1.5 * jax.random.uniform(keys[8], (HEADS,), jnp.float32) ** levels(keys[8], (HEADS,), ((0, 8),), -0.2, 0.2), 0.5, 2.0)
    norm_gain = jnp.clip(1.0 + 0.1 * jax.random.normal(keys[9], (INNER,), jnp.float32), 0.5, 1.5)
    readout = normal_values(keys[10], (INNER,), INNER ** -0.5, 0.0625, ((0, 8),))
    lengths = uneven_parts(keys[11], CANDS, TOKENS, TOKENS // 2, 2).astype(jnp.int32)
    return dict(x_in=x_in, gate_z=gate_z, bc_in=bc_in, dt_raw=dt_raw, conv_x=conv_x, conv_bc=conv_bc, dt_bias=dt_bias, a_log=a_log, d_skip=d_skip, norm_gain=norm_gain, readout=readout, lengths=lengths)


HIGHEST_PREC = lax.Precision.HIGHEST

def segment_of(positions, lengths):
    offsets = (jnp.cumsum(lengths) - lengths).astype(jnp.int32)
    return (lax.optimization_barrier(jnp.sum((positions[:, None] >= offsets[None, :]).astype(jnp.int32), axis=1)) - 1).astype(jnp.int32)

def causal_conv(extended, weights, seg_ext):
    span_count = seg_ext.shape[0] - 3
    seg_now = seg_ext[3:]
    conv_sum = jnp.zeros((span_count, extended.shape[1]), jnp.float32)
    for lag_index in range(4):
        same_doc = (seg_ext[3 - lag_index:3 - lag_index + span_count] == seg_now).astype(jnp.float32)
        piece_in = extended[3 - lag_index:3 - lag_index + span_count].astype(jnp.float32)
        conv_sum = conv_sum + weights[lag_index][None, :] * piece_in * same_doc[:, None]
    return jax.nn.silu(conv_sum)

def block_ssd(x_conv, b_mat, c_mat, dt_vals, decay_log, segment, seg_before, ssd_state, d_skip):
    per_group = x_conv.shape[1] // b_mat.shape[1]
    cumulative = jnp.cumsum(decay_log, axis=0)
    cb_scores = jnp.einsum('tgn,sgn->gts', c_mat, b_mat, precision=HIGHEST_PREC)
    cb_scores = jnp.repeat(cb_scores, per_group, axis=0)
    order_row = jnp.arange(segment.shape[0])
    inside = (segment[:, None] == segment[None, :]) & (order_row[:, None] >= order_row[None, :])
    gap_log = cumulative.T[:, :, None] - cumulative.T[:, None, :]
    weights_mat = jnp.exp(jnp.where(inside[None], gap_log, -jnp.inf)) * cb_scores * dt_vals.T[:, None, :]
    within = jnp.einsum('hts,shp->thp', weights_mat, x_conv, precision=HIGHEST_PREC)
    c_head = jnp.repeat(c_mat, per_group, axis=1)
    b_head = jnp.repeat(b_mat, per_group, axis=1)
    alive_mask = (segment == seg_before).astype(jnp.float32)
    carried = jnp.einsum('thn,hpn->thp', c_head, ssd_state, precision=HIGHEST_PREC)
    carried = carried * (jnp.exp(cumulative) * alive_mask[:, None])[:, :, None]
    result_y = within + carried + d_skip[None, :, None] * x_conv
    tail_weight = jnp.exp(cumulative[-1][None, :] - cumulative) * (segment == segment[-1]).astype(jnp.float32)[:, None] * dt_vals
    fresh_state = jnp.einsum('shp,shn->hpn', tail_weight[:, :, None] * x_conv, b_head, precision=HIGHEST_PREC)
    new_state = fresh_state + (jnp.exp(cumulative[-1]) * alive_mask[-1])[:, None, None] * ssd_state
    return (result_y, new_state)

def gated_norm(values, gate_in, gain_vec, groups):
    gated = values * jax.nn.silu(gate_in.astype(jnp.float32))
    grouped = gated.reshape(gated.shape[0], groups, -1)
    inv_scale = lax.rsqrt(lax.optimization_barrier(jnp.mean(grouped * grouped, axis=2, keepdims=True)) + 1e-05)
    return ((grouped * inv_scale).reshape(gated.shape) * gain_vec[None, :]).astype(jnp.bfloat16)

def reference(x_in, gate_z, bc_in, dt_raw, conv_x, conv_bc, dt_bias, a_log, d_skip, norm_gain, readout, lengths):
    token_count, inner_width = x_in.shape
    head_count = dt_raw.shape[1]
    groups = bc_in.shape[1]
    state_size = bc_in.shape[2] // 2
    head_dim = inner_width // head_count
    block_count = token_count // STRETCH
    positions = jnp.arange(token_count, dtype=jnp.int32)
    segment = segment_of(positions, lengths)
    dt_vals = jax.nn.softplus(dt_raw + dt_bias[None, :])
    decay_log = -dt_vals * jnp.exp(a_log)[None, :]
    weights_bc = conv_bc.reshape(4, groups * 2 * state_size)
    bc_flat = bc_in.reshape(token_count, groups * 2 * state_size)

    def block_step(carry_in, block_in):
        ssd_state, tail_x, tail_bc, tail_seg = carry_in
        x_blk, z_blk, bc_blk, dt_blk, dl_blk, seg_blk = block_in
        seg_ext = jnp.concatenate([tail_seg, seg_blk])
        x_conv = causal_conv(jnp.concatenate([tail_x, x_blk]), conv_x, seg_ext)
        bc_conv = causal_conv(jnp.concatenate([tail_bc, bc_blk]), weights_bc, seg_ext)
        bc_conv = bc_conv.reshape(-1, groups, 2 * state_size)
        result_y, ssd_state = block_ssd(x_conv.reshape(-1, head_count, head_dim), bc_conv[:, :, :state_size], bc_conv[:, :, state_size:], dt_blk, dl_blk, seg_blk, tail_seg[2], ssd_state, d_skip)
        mixed_blk = gated_norm(result_y.reshape(-1, inner_width), z_blk, norm_gain, groups)
        return ((ssd_state, x_blk[-3:], bc_blk[-3:], seg_blk[-3:]), mixed_blk)
    carry_start = (jnp.zeros((head_count, head_dim, state_size), jnp.float32), jnp.zeros((3, inner_width), jnp.bfloat16), jnp.zeros((3, groups * 2 * state_size), jnp.bfloat16), jnp.full((3,), -1, jnp.int32))
    blocks_in = (x_in.reshape(block_count, STRETCH, inner_width), gate_z.reshape(block_count, STRETCH, inner_width), bc_flat.reshape(block_count, STRETCH, -1), dt_vals.reshape(block_count, STRETCH, head_count), decay_log.reshape(block_count, STRETCH, head_count), segment.reshape(block_count, STRETCH))
    _, mixed_blocks = lax.scan(block_step, carry_start, blocks_in)
    mixed_out = mixed_blocks.reshape(token_count, inner_width)
    cand_ends = (jnp.cumsum(lengths) - 1).astype(jnp.int32)
    picked = mixed_out[cand_ends]
    cand_scores = jnp.dot(picked, readout, preferred_element_type=jnp.float32)
    return (mixed_out, cand_scores)
```

```python
import functools

import jax
import jax.numpy as jnp
from jax import lax
from jax.experimental import pallas as pl
from jax.experimental.pallas import tpu as pltpu
from jax.sharding import PartitionSpec as P

F32, BF16, I32 = jnp.float32, jnp.bfloat16, jnp.int32
MESH = pl.DeviceIdType.MESH
LOG2E = 1.4426950408889634
Q = 128
QW = 256
HALO = 16
RESET = 200.0
LANES = 128
CHUNK_ROWS = 16


def iota(shape, dim):
    return lax.broadcasted_iota(I32, shape, dim)


def dot(a, b):
    return jnp.dot(a, b, preferred_element_type=F32)


def three(x):
    hi = x.astype(BF16)
    rest = x - hi.astype(F32)
    mid = rest.astype(BF16)
    return hi, mid, (rest - mid.astype(F32)).astype(BF16)


def softplus(v):
    u = jnp.exp(-jnp.abs(v))
    small = u * (1.0 + u * (-0.5 + u * (1.0 / 3.0 - 0.25 * u)))
    return jnp.maximum(v, 0.0) + jnp.where(u < 0.01, small, jnp.log(1.0 + u))


def twice_silu_half(h):
    return h + h * jnp.tanh(h)


def conv_block(rows, before, taps, shift, near):
    width = rows.shape[1]
    scaled = jnp.concatenate([rows * tap.astype(BF16) for tap in taps], axis=0)
    out = dot(shift, scaled)
    tail = before.astype(F32)[8:16]
    row = iota((8, width), 0)
    first = jnp.zeros((8, width), F32)
    near = jnp.concatenate([near] * (width // LANES), axis=1)
    for lag in (1, 2, 3):
        first = first + jnp.where(
            (row < lag) & (near >= lag), pltpu.roll(tail, lag, 0) * taps[lag], 0.0
        )
    return jnp.concatenate([out[:8] + first, out[8:]], axis=0)


def kernel(
    dims,
    lengths, bias, a_log, d_skip,
    dt_ref, conv_x, conv_bc, gain, readout, x_hbm, z_hbm, bc_hbm,
    out_hbm, score_ref,
    xq, bcs, zq, hx, hbc, shift, pos8, cols, colf, vrow, tots, dec_blk, dec_pre, sel_w, sel_e,
    xc, cmat, btr, cb, sk, state, sbuf, ypre, gated, stage, score_acc,
    my_dec, got_dec, got_s, ret_s, inbound, sc_mine, sc_ctx, got_h, got_c,
    sem_x, sem_bc, sem_z, sem_out, sem_halo_s, sem_halo_r, sem_s, sem_r,
):
    n_ctx, n_head, rows_all, heads, split = dims
    blocks = rows_all // Q
    quads = heads * 64 // QW
    pairs = heads // 2
    many = n_ctx > 1
    me = lax.axis_index("ctx")
    me_head = lax.axis_index("head")
    part_rows = Q // 4
    plane, lane_y = me // 4, me % 4

    if many:
        barrier = pltpu.get_barrier_semaphore()

        def greet_ctx(i, _):
            pl.semaphore_signal(barrier, inc=1, device_id={"ctx": lax.rem(me + i, n_ctx)}, device_id_type=MESH)
            return 0

        lax.fori_loop(1, n_ctx, greet_ctx, 0)

        def greet_head(i, _):
            pl.semaphore_signal(barrier, inc=1, device_id={"head": lax.rem(me_head + i, n_head)}, device_id_type=MESH)
            return 0

        lax.fori_loop(1, n_head, greet_head, 0)

    load_bc = pltpu.make_async_copy(bc_hbm, bcs, sem_bc)
    load_bc.start()
    load_x = [
        pltpu.make_async_copy(x_hbm.at[:, pl.ds(q * QW, QW)], xq.at[q], sem_x.at[q])
        for q in range(quads)
    ]
    load_z = [
        pltpu.make_async_copy(z_hbm.at[:, pl.ds(q * QW, QW)], zq.at[q], sem_z.at[q])
        for q in range(quads)
    ]
    for copy in load_x:
        copy.start()
    for copy in load_z:
        copy.start()

    offset = jnp.int32(0)
    here = me * rows_all + iota((CHUNK_ROWS, LANES), 0) * Q + iota((CHUNK_ROWS, LANES), 1)
    since = jnp.full((CHUNK_ROWS, LANES), 1 << 20, I32)
    ends = jnp.zeros((CHUNK_ROWS, LANES), I32)
    for c in range(lengths.shape[0]):
        gone = here - offset
        since = jnp.where(gone >= 0, jnp.minimum(since, gone), since)
        offset = offset + lengths[c]
        ends = jnp.where(iota((CHUNK_ROWS, LANES), 0) == c, offset - 1, ends)
    since = since.astype(F32)
    near = jnp.minimum(since, 3.0)

    head_row = iota((heads, LANES), 0)
    bias_col = jnp.zeros((heads, LANES), F32)
    rate_col = jnp.zeros((heads, LANES), F32)
    for h in range(heads):
        bias_col = jnp.where(head_row == h, bias[h], bias_col)
        rate_col = jnp.where(head_row == h, a_log[h], rate_col)
    rate_col = jnp.exp(rate_col) * (-LOG2E)
    steps, logs = [], []
    for k in range(blocks):
        dt_vals = softplus(dt_ref[:, k * Q : (k + 1) * Q] + bias_col)
        steps.append(jnp.log(dt_vals) * LOG2E)
        fresh = jnp.where(since[k : k + 1] == 0.0, RESET, 0.0)
        logs.append(dt_vals * rate_col - fresh)
    upper = (iota((Q, Q), 0) <= iota((Q, Q), 1)).astype(F32).astype(BF16)
    cum_all = dot(
        jnp.concatenate(three(jnp.concatenate(logs, axis=0)), axis=1),
        jnp.concatenate([upper] * 3, axis=0),
    )
    before = jnp.zeros((heads, LANES), F32)
    for k in range(blocks):
        cum = cum_all[k * heads : (k + 1) * heads]
        value = steps[k] - cum
        total = jnp.broadcast_to(cum[:, Q - 1 : Q], (heads, LANES))
        vrow[k] = value
        tots[2 * k] = total
        tots[2 * k + 1] = before
        before = before + total
        tile = jnp.concatenate(
            [cum, jnp.exp2(cum), jnp.exp2(total + value), near, jnp.zeros((Q - 64, LANES), F32)], axis=0
        )
        tile = tile.T
        colf[k] = tile
        hi = tile.astype(BF16)
        cols[k] = jnp.concatenate([hi, (tile - hi.astype(F32)).astype(BF16)], axis=1)
    tots[2 * blocks] = before
    left = iota((pairs, LANES), 1) < 64

    def by_pair(i):
        return jnp.exp2(
            jnp.where(left, tots[i, pl.ds(0, pairs, stride=2), :], tots[i, pl.ds(1, pairs, stride=2), :])
        )

    for k in range(blocks):
        dec_blk[k] = by_pair(2 * k)
        dec_pre[k] = by_pair(2 * k + 1)
    dec_all = by_pair(2 * blocks)
    for p in range(pairs):
        my_dec[p] = dec_all[p : p + 1]

    sel_row = iota((2 * Q, heads * 64), 0)
    sel_head = iota((2 * Q, heads * 64), 1) // 64
    sel_w[...] = ((sel_row == sel_head + 2 * heads) | (sel_row == sel_head + 2 * heads + Q)).astype(F32).astype(BF16)
    sel_e[...] = ((sel_row == sel_head + heads) | (sel_row == sel_head + heads + Q)).astype(F32).astype(BF16)
    row_q, col_q = iota((Q, Q), 0), iota((Q, Q), 1)
    for k in range(blocks):
        reach = jnp.broadcast_to(colf[k, :, 3 * heads + k : 3 * heads + k + 1], (Q, Q))
        pos8[k] = reach[:8]
        shift[k] = jnp.concatenate(
            [
                jnp.where((col_q == row_q - lag) & (reach >= lag), 1.0, 0.0).astype(BF16)
                for lag in range(4)
            ],
            axis=1,
        )

    nxt = lax.rem(me + 1, n_ctx)
    if many:
        pl.semaphore_wait(barrier, n_ctx - 1 + n_head - 1)
        halo_x = pltpu.make_async_remote_copy(
            src_ref=x_hbm.at[pl.ds(rows_all - HALO, HALO), :], dst_ref=hx,
            send_sem=sem_halo_s.at[0], recv_sem=sem_halo_r.at[0],
            device_id={"ctx": nxt}, device_id_type=MESH,
        )
        halo_bc = pltpu.make_async_remote_copy(
            src_ref=bc_hbm.at[pl.ds(rows_all - HALO, HALO), :], dst_ref=hbc,
            send_sem=sem_halo_s.at[1], recv_sem=sem_halo_r.at[1],
            device_id={"ctx": nxt}, device_id_type=MESH,
        )
        halo_x.start()
        halo_bc.start()

        def send_dec(i, _):
            other = lax.rem(me + i, n_ctx)
            pltpu.make_async_remote_copy(
                src_ref=my_dec.at[other // 4], dst_ref=got_dec.at[me],
                send_sem=sem_s.at[0], recv_sem=sem_r.at[0],
                device_id={"ctx": other}, device_id_type=MESH,
            ).start()
            return 0

        lax.fori_loop(1, n_ctx, send_dec, 0)
        got_dec[me] = my_dec[plane]
    else:
        hx[...] = jnp.zeros_like(hx)
        hbc[...] = jnp.zeros_like(hbc)

    load_bc.wait()
    if many:
        halo_bc.wait()
    causal = row_q >= col_q
    bc_taps = [conv_bc[lag] * 0.5 for lag in range(4)]
    for k in range(blocks):
        prev = hbc[...] if k == 0 else bcs[k * Q - HALO : k * Q, :]
        half = conv_block(bcs[k * Q : (k + 1) * Q, :], prev, bc_taps, shift[k], pos8[k])
        bc = twice_silu_half(half)
        b_t = bc[:, :LANES].T.astype(BF16)
        c_mat = bc[:, LANES:].astype(BF16)
        btr[k] = b_t
        cmat[k] = c_mat
        cb[k] = jnp.where(causal, dot(c_mat, b_t), 0.0).astype(BF16)

    for copy in load_x:
        copy.wait()
    if many:
        halo_x.wait()

    def one_quad(i, _):
        q = lax.rem(plane // 2 + i, quads) if many else i
        at = pl.multiple_of(q * QW, QW)
        taps = [conv_x[lag : lag + 1, pl.ds(at, QW)] * 0.5 for lag in range(4)]
        sel = sel_w[:, pl.ds(at, QW)]
        held = jnp.zeros((LANES, QW), F32)
        for k in range(blocks):
            prev = hx[:, pl.ds(at, QW)] if k == 0 else xq[q, k * Q - HALO : k * Q, :]
            half = conv_block(xq[q, k * Q : (k + 1) * Q, :], prev, taps, shift[k], pos8[k])
            act = twice_silu_half(half)
            xc[q, k * Q : (k + 1) * Q, :] = act.astype(BF16)
            weighed = (act * dot(cols[k], sel)).astype(BF16)
            sk[q, k] = held.astype(BF16)
            dec = jnp.concatenate([dec_blk[k, pl.ds(2 * q, 1), :], dec_blk[k, pl.ds(2 * q + 1, 1), :]], axis=1)
            held = held * dec + dot(btr[k], weighed)
        if many:
            for side in range(2):
                p = 2 * q + side
                sbuf[p] = held[:, side * LANES : (side + 1) * LANES].astype(BF16)
                for part in range(4):
                    owner = p * 4 + part

                    @pl.when(owner != me)
                    def _():
                        pltpu.make_async_remote_copy(
                            src_ref=sbuf.at[p, pl.ds(part * part_rows, part_rows), :], dst_ref=got_s.at[me],
                            send_sem=sem_s.at[1], recv_sem=sem_r.at[1],
                            device_id={"ctx": owner}, device_id_type=MESH,
                        ).start()

                    @pl.when(owner == me)
                    def _():
                        got_s[me] = sbuf[p, part * part_rows : (part + 1) * part_rows, :]

        return 0

    lax.fori_loop(0, quads, one_quad, 0)

    for copy in load_z:
        copy.wait()
    left_bf = iota((Q, LANES), 1) < 64

    def one_block(k, _):
        rows = pl.ds(pl.multiple_of(k * Q, Q), Q)
        cb_k = cb[k]
        for q in range(quads):
            out = []
            for side in range(2):
                pair = 2 * q + side
                weights = []
                for h in (2 * pair, 2 * pair + 1):
                    gap = colf[k, :, h : h + 1] + vrow[k, h : h + 1, :]
                    fade = jnp.where(causal, jnp.exp2(gap), 0.0).astype(BF16)
                    weights.append(fade * cb_k)
                x_pair = xc[q, rows, side * LANES : (side + 1) * LANES]
                zero = jnp.zeros_like(x_pair)
                both = jnp.concatenate([jnp.where(left_bf, x_pair, zero), jnp.where(left_bf, zero, x_pair)], axis=0)
                skip = jnp.where(iota((1, LANES), 1) < 64, d_skip[2 * pair], d_skip[2 * pair + 1])
                out.append(dot(jnp.concatenate(weights, axis=1), both) + skip * x_pair.astype(F32))
            ypre[q, rows, :] = jnp.concatenate(out, axis=1)
            z_half = zq[q, rows, :].astype(F32) * 0.5
            gated[q, rows, :] = twice_silu_half(z_half)
        return 0

    lax.fori_loop(0, split, one_block, 0)

    def all_of(sem, like, count):
        view = like.at[pl.ds(0, count)]
        pltpu.make_async_copy(view, view, sem).wait()

    if many:
        all_of(sem_r.at[0], got_dec, n_ctx - 1)
        all_of(sem_r.at[1], got_s, n_ctx - 1)

        def lap(d, acc):
            ret_s[d] = acc.astype(BF16)
            return acc * got_dec[d] + got_s[d].astype(F32)

        lax.fori_loop(0, n_ctx, lap, jnp.zeros((part_rows, LANES), F32), unroll=True)

        def send_back(i, _):
            other = lax.rem(me + i, n_ctx)
            pltpu.make_async_remote_copy(
                src_ref=ret_s.at[other],
                dst_ref=inbound.at[plane, lane_y],
                send_sem=sem_s.at[2], recv_sem=sem_r.at[2],
                device_id={"ctx": other}, device_id_type=MESH,
            ).start()
            return 0

        lax.fori_loop(1, n_ctx, send_back, 0)
        inbound[plane, lane_y] = ret_s[me]

    lax.fori_loop(split, blocks, one_block, 0)

    if many:
        pltpu.make_async_copy(ret_s.at[pl.ds(0, n_ctx - 1)], ret_s.at[pl.ds(0, n_ctx - 1)], sem_r.at[2]).wait()
    else:
        inbound[...] = jnp.zeros_like(inbound)

    score_acc[...] = jnp.zeros_like(score_acc)
    gain_row = gain[...]

    def finish(k, _):
        rows = pl.ds(pl.multiple_of(k * Q, Q), Q)
        squares = jnp.zeros((Q, LANES), F32)
        for q in range(quads):
            dec = jnp.concatenate([dec_pre[k, 2 * q : 2 * q + 1, :], dec_pre[k, 2 * q + 1 : 2 * q + 2, :]], axis=1)
            came = jnp.concatenate(
                [inbound[2 * q].reshape(LANES, LANES), inbound[2 * q + 1].reshape(LANES, LANES)], axis=1
            ).astype(F32)
            start = (sk[q, k].astype(F32) + dec * came).astype(BF16)
            carried = dot(cmat[k], start) * dot(cols[k], sel_e[:, q * QW : (q + 1) * QW])
            value = (ypre[q, rows, :] + carried) * gated[q, rows, :]
            ypre[q, rows, :] = value
            square = value * value
            squares = squares + square[:, :LANES] + square[:, LANES:]
        inv = lax.rsqrt(jnp.sum(squares, axis=1, keepdims=True) * (1.0 / (heads * 64)) + 1e-05)
        for q in range(quads):
            mixed = ypre[q, rows, :] * inv * gain_row[:, q * QW : (q + 1) * QW]
            stage[rows, q * QW : (q + 1) * QW] = mixed.astype(BF16)
        pltpu.make_async_copy(stage.at[rows, :], out_hbm.at[rows, :], sem_out).start()
        spot = me * rows_all + k * Q + iota((CHUNK_ROWS, LANES), 1)
        pick = jnp.where(ends == spot, 1.0, 0.0).astype(BF16)
        score_acc[...] += dot(pick, stage[rows, :])
        return 0

    lax.fori_loop(0, blocks, finish, 0)

    score = jnp.sum(score_acc[...] * readout[...].astype(F32), axis=1, keepdims=True)
    diag = iota((CHUNK_ROWS, LANES), 0) == iota((CHUNK_ROWS, LANES), 1)
    score_row = jnp.sum(jnp.where(diag, score, 0.0), axis=0, keepdims=True)
    if many:
        sc_mine[0] = score_row

        def to_head(i, _):
            other = lax.rem(me_head + i, n_head)
            pltpu.make_async_remote_copy(
                src_ref=sc_mine.at[0], dst_ref=got_h.at[me_head],
                send_sem=sem_s.at[3], recv_sem=sem_r.at[3],
                device_id={"head": other}, device_id_type=MESH,
            ).start()
            return 0

        lax.fori_loop(1, n_head, to_head, 0)
        got_h[me_head] = score_row
        all_of(sem_r.at[3], got_h, n_head - 1)
        score_row = jnp.sum(got_h[...], axis=0)
        sc_ctx[0] = score_row

        def to_ctx(i, _):
            other = lax.rem(me + i, n_ctx)
            pltpu.make_async_remote_copy(
                src_ref=sc_ctx.at[0], dst_ref=got_c.at[me],
                send_sem=sem_s.at[4], recv_sem=sem_r.at[4],
                device_id={"ctx": other}, device_id_type=MESH,
            ).start()
            return 0

        lax.fori_loop(1, n_ctx, to_ctx, 0)
        got_c[me] = score_row
        all_of(sem_r.at[4], got_c, n_ctx - 1)
        score_row = jnp.sum(got_c[...], axis=0)
        all_of(sem_s.at[0], got_dec, n_ctx - 1)
        all_of(sem_s.at[1], got_s, n_ctx - 1)
        all_of(sem_s.at[2], got_s, n_ctx - 1)
        all_of(sem_s.at[3], got_h, n_head - 1)
        all_of(sem_s.at[4], got_c, n_ctx - 1)
    score_ref[...] = score_row
    pltpu.make_async_copy(stage, out_hbm, sem_out).wait()


def local(n_ctx, n_head, x_in, gate_z, bc_in, dt_raw, conv_x, conv_bc, dt_bias, a_log, d_skip, norm_gain, readout, lengths):
    rows, width = x_in.shape
    heads = dt_raw.shape[1]
    blocks, quads, pairs = rows // Q, width // QW, heads // 2
    smem = pl.BlockSpec(memory_space=pltpu.SMEM)
    vmem = pl.BlockSpec(memory_space=pltpu.VMEM)
    hbm = pl.BlockSpec(memory_space=pl.ANY)
    dma = pltpu.SemaphoreType.DMA
    scratch = [
        pltpu.VMEM((quads, rows, QW), BF16),
        pltpu.VMEM((rows, 256), BF16),
        pltpu.VMEM((quads, rows, QW), BF16),
        pltpu.VMEM((HALO, width), BF16),
        pltpu.VMEM((HALO, 256), BF16),
        pltpu.VMEM((blocks, Q, 4 * Q), BF16),
        pltpu.VMEM((blocks, 8, LANES), F32),
        pltpu.VMEM((blocks, Q, 2 * Q), BF16),
        pltpu.VMEM((blocks, Q, Q), F32),
        pltpu.VMEM((blocks, heads, LANES), F32),
        pltpu.VMEM((2 * blocks + 1, heads, LANES), F32),
        pltpu.VMEM((blocks, pairs, LANES), F32),
        pltpu.VMEM((blocks, pairs, LANES), F32),
        pltpu.VMEM((2 * Q, width), BF16),
        pltpu.VMEM((2 * Q, width), BF16),
        pltpu.VMEM((quads, rows, QW), BF16),
        pltpu.VMEM((blocks, Q, LANES), BF16),
        pltpu.VMEM((blocks, LANES, Q), BF16),
        pltpu.VMEM((blocks, Q, Q), BF16),
        pltpu.VMEM((quads, blocks, LANES, QW), BF16),
        pltpu.VMEM((LANES, QW), F32),
        pltpu.VMEM((pairs, LANES, LANES), BF16),
        pltpu.VMEM((quads, rows, QW), F32),
        pltpu.VMEM((quads, rows, QW), F32),
        pltpu.VMEM((rows, width), BF16),
        pltpu.VMEM((CHUNK_ROWS, width), F32),
        pltpu.VMEM((pairs, 1, LANES), F32),
        pltpu.VMEM((n_ctx, 1, LANES), F32),
        pltpu.VMEM((n_ctx, Q // 4, LANES), BF16),
        pltpu.VMEM((n_ctx, Q // 4, LANES), BF16),
        pltpu.VMEM((pairs, 4, Q // 4, LANES), BF16),
        pltpu.VMEM((1, 1, LANES), F32),
        pltpu.VMEM((1, 1, LANES), F32),
        pltpu.VMEM((n_head, 1, LANES), F32),
        pltpu.VMEM((n_ctx, 1, LANES), F32),
        dma((quads,)), dma, dma((quads,)), dma, dma((2,)), dma((2,)), dma((5,)), dma((5,)),
    ]
    params = dict(vmem_limit_bytes=60 * 1024 * 1024)
    if n_ctx > 1:
        params.update(collective_id=0, has_side_effects=True)
    split = min(4, blocks)
    mixed, score = pl.pallas_call(
        functools.partial(kernel, (n_ctx, n_head, rows, heads, split)),
        out_shape=(jax.ShapeDtypeStruct((rows, width), BF16), jax.ShapeDtypeStruct((1, LANES), F32)),
        in_specs=[smem] * 4 + [vmem] * 5 + [hbm] * 3,
        out_specs=(hbm, vmem),
        scratch_shapes=scratch,
        compiler_params=pltpu.CompilerParams(**params),
    )(
        lengths, dt_bias, a_log, d_skip,
        dt_raw.T, conv_x, conv_bc, norm_gain.reshape(1, width), readout.reshape(1, width),
        x_in, gate_z, bc_in.reshape(rows, bc_in.shape[2]),
    )
    return mixed, score.reshape(LANES)[: lengths.shape[0]]


def solution(mesh):
    in_specs = (
        P("ctx", "head"),
        P("ctx", "head"),
        P("ctx", "head", None),
        P("ctx", "head"),
        P(None, "head"),
        P(None, "head", None),
        P("head"),
        P("head"),
        P("head"),
        P("head"),
        P("head"),
        P(),
    )
    out_specs = (P("ctx", "head"), P())
    step = functools.partial(local, mesh.shape["ctx"], mesh.shape["head"])
    return jax.shard_map(step, mesh=mesh, in_specs=in_specs, out_specs=out_specs, check_vma=False)
```

```python
import functools

import jax
import jax.numpy as jnp
from jax import lax
from jax.experimental import pallas as pl
from jax.experimental.pallas import tpu as pltpu
from jax.sharding import PartitionSpec as P

F32, BF16, I32 = jnp.float32, jnp.bfloat16, jnp.int32
MESH = pl.DeviceIdType.MESH
LOG2E = 1.4426950408889634
Q = 128
QW = 256
HALO = 16
RESET = 200.0
LANES = 128
TABLE = 16
PART = 32
MSG = PART + 16


def iota(shape, dim):
    return lax.broadcasted_iota(I32, shape, dim)


def dot(a, b):
    return jnp.dot(a, b, preferred_element_type=F32)


def dot_t(a, b):
    return lax.dot_general(a, b, (((0,), (0,)), ((), ())), preferred_element_type=F32)


def two(x):
    hi = x.astype(BF16)
    return hi, (x - hi.astype(F32)).astype(BF16)


def three(x):
    hi = x.astype(BF16)
    return (hi,) + two(x - hi.astype(F32))


def softplus(v):
    u = jnp.exp(-jnp.abs(v))
    small = u * (1.0 + u * (-0.5 + u * (1.0 / 3.0 - 0.25 * u)))
    return jnp.maximum(v, 0.0) + jnp.where(u < 0.01, small, jnp.log(1.0 + u))


def twice_silu_half(h):
    return h + h * jnp.tanh(h)


def half_conv(rows, before, taps, keep):
    x = jnp.concatenate([before.astype(F32)[HALO - 8 :], rows.astype(F32)], axis=0)
    keep = jnp.concatenate([keep] * (x.shape[1] // LANES), axis=1)
    acc = x * taps[3]
    for lag in (2, 1, 0):
        acc = pltpu.roll(acc, 1, 0) * keep + x * taps[lag]
    return acc[8:]


def kernel(
    dims,
    lengths_hbm, bias_hbm, a_log_hbm, d_skip_hbm,
    dt_hbm, conv_x_hbm, conv_bc_hbm, gain_hbm, readout_hbm, x_hbm, z_hbm, bc_hbm,
    out_hbm, score_ref,
    lengths, bias, a_log, d_skip, dt_ref, conv_x, conv_bc, gain, readout,
    xq, bcs, zq, hx, hbc, keep, colf, vrow, whl, ehl, tots, dec_blk, dec_pre, sel,
    xc, cmat, cwide, btr, cb, sk, fresh, dec_one, sbuf, part_a, part_b, stage, sin, end_a, end_b, end_c,
    got_s, ret_s, inbound, sc_mine, sc_ctx, got_h, got_c,
    sem_small, sem_x, sem_bc, sem_z, sem_out, sem_halo_s, sem_halo_r, sem_s, sem_r,
):
    n_ctx, n_head, rows_all, heads, split = dims
    blocks = rows_all // Q
    quads = heads * 64 // QW
    pairs = heads // 2
    many = n_ctx > 1
    me = lax.axis_index("ctx")
    me_head = lax.axis_index("head")
    plane, lane_y = me // 4, me % 4

    load_small = [
        pltpu.make_async_copy(source, target, sem_small.at[i])
        for i, (source, target) in enumerate(
            [
                (lengths_hbm, lengths), (bias_hbm, bias), (a_log_hbm, a_log), (d_skip_hbm, d_skip),
                (dt_hbm, dt_ref), (conv_x_hbm, conv_x), (conv_bc_hbm, conv_bc), (gain_hbm, gain), (readout_hbm, readout),
            ]
        )
    ]
    for copy in load_small:
        copy.start()
    load_bc = pltpu.make_async_copy(bc_hbm, bcs, sem_bc)
    load_bc.start()
    load_x = [
        pltpu.make_async_copy(x_hbm.at[:, pl.ds(q * QW, QW)], xq.at[q], sem_x.at[q])
        for q in range(quads)
    ]
    load_z = [
        pltpu.make_async_copy(z_hbm.at[:, pl.ds(q * QW, QW)], zq.at[q], sem_z.at[q])
        for q in range(quads)
    ]
    for copy in load_x + load_z:
        copy.start()

    if many:
        barrier = pltpu.get_barrier_semaphore()

        def greet_ctx(i, _):
            pl.semaphore_signal(barrier, inc=1, device_id={"ctx": lax.rem(me + i, n_ctx)}, device_id_type=MESH)
            return 0

        lax.fori_loop(1, n_ctx, greet_ctx, 0)

        def greet_head(i, _):
            pl.semaphore_signal(barrier, inc=1, device_id={"head": lax.rem(me_head + i, n_head)}, device_id_type=MESH)
            return 0

        lax.fori_loop(1, n_head, greet_head, 0)

    for copy in load_small:
        copy.wait()

    offset = jnp.int32(0)
    here = me * rows_all + (iota((TABLE, LANES), 0) - 1) * Q + iota((TABLE, LANES), 1)
    first = jnp.zeros((TABLE, LANES), F32)
    ends = []
    for c in range(lengths.shape[0]):
        first = jnp.where(here == offset, 1.0, first)
        offset = offset + lengths[c]
        ends.append(offset - 1)

    head_row = iota((heads, LANES), 0)
    bias_col = jnp.zeros((heads, LANES), F32)
    rate_col = jnp.zeros((heads, LANES), F32)
    for h in range(heads):
        bias_col = jnp.where(head_row == h, bias[h], bias_col)
        rate_col = jnp.where(head_row == h, a_log[h], rate_col)
    rate_col = jnp.exp(rate_col) * (-LOG2E)
    steps, logs = [], []
    for k in range(blocks):
        dt_vals = softplus(dt_ref[:, k * Q : (k + 1) * Q] + bias_col)
        steps.append(jnp.log(dt_vals) * LOG2E)
        logs.append(dt_vals * rate_col - RESET * first[k + 1 : k + 2])
    upper = (iota((Q, Q), 0) <= iota((Q, Q), 1)).astype(F32).astype(BF16)
    cum_all = dot(
        jnp.concatenate(three(jnp.concatenate(logs, axis=0)), axis=1),
        jnp.concatenate([upper] * 3, axis=0),
    )
    before = jnp.zeros((heads, LANES), F32)
    for k in range(blocks):
        cum = cum_all[k * heads : (k + 1) * heads]
        value = steps[k] - cum
        total = jnp.broadcast_to(cum[:, Q - 1 : Q], (heads, LANES))
        vrow[k] = value
        colf[k, :heads] = cum
        whl[k] = jnp.concatenate(two(jnp.exp2(total + value)), axis=0)
        tots[2 * k] = total
        tots[2 * k + 1] = before
        before = before + total
    tots[2 * blocks] = before
    left = iota((pairs, LANES), 1) < 64

    def by_pair(i):
        return jnp.where(left, tots[i, pl.ds(0, pairs, stride=2), :], tots[i, pl.ds(1, pairs, stride=2), :])

    one_on = by_pair(3)
    for k in range(blocks):
        dec_blk[k] = jnp.exp2(by_pair(2 * k))
    dec_one[blocks] = jnp.exp2(by_pair(2 * blocks) - one_on)

    sel_row, sel_head = iota((2 * heads, heads * 64), 0), iota((2 * heads, heads * 64), 1) // 64
    sel[...] = jnp.where((sel_row == sel_head) | (sel_row == sel_head + heads), 1.0, 0.0).astype(BF16)
    keep_col = jnp.concatenate([1.0 - first, jnp.zeros((LANES - TABLE, LANES), F32)], axis=0).T
    for k in range(blocks + 1):
        keep[k * Q : (k + 1) * Q, :] = jnp.broadcast_to(keep_col[:, k : k + 1], (Q, LANES))

    load_bc.wait()
    bc_taps = [conv_bc[lag] * 0.5 for lag in range(4)]

    def conv_bc_block(k, at):
        prev = hbc[:, at : at + LANES] if k == 0 else bcs[k * Q - HALO : k * Q, at : at + LANES]
        half = half_conv(
            bcs[k * Q : (k + 1) * Q, at : at + LANES], prev,
            [tap[:, at : at + LANES] for tap in bc_taps], keep[(k + 1) * Q - 8 : (k + 2) * Q, :],
        )
        return twice_silu_half(half)

    if many:
        dec_all = jnp.exp2(by_pair(2 * blocks))
        part_row = iota((16, LANES), 0)
        for p in range(pairs):
            hi, mid, low = (v.astype(F32) for v in three(dec_all[p : p + 1]))
            tile = jnp.where(part_row == 0, hi, jnp.where(part_row == 1, mid, jnp.where(part_row == 2, low, 0.0)))
            for part in range(4):
                sbuf[p, part, PART:, :] = tile.astype(BF16)

    for k in range(1, blocks):
        btr[k] = conv_bc_block(k, 0).T.astype(BF16)

    nxt = lax.rem(me + 1, n_ctx)
    if many:
        pl.semaphore_wait(barrier, n_ctx - 1 + n_head - 1)
        halo_x = pltpu.make_async_remote_copy(
            src_ref=x_hbm.at[pl.ds(rows_all - HALO, HALO), :], dst_ref=hx,
            send_sem=sem_halo_s.at[0], recv_sem=sem_halo_r.at[0],
            device_id={"ctx": nxt}, device_id_type=MESH,
        )
        halo_bc = pltpu.make_async_remote_copy(
            src_ref=bc_hbm.at[pl.ds(rows_all - HALO, HALO), :], dst_ref=hbc,
            send_sem=sem_halo_s.at[1], recv_sem=sem_halo_r.at[1],
            device_id={"ctx": nxt}, device_id_type=MESH,
        )
        halo_x.start()
        halo_bc.start()
    else:
        hx[...] = jnp.zeros_like(hx)
        hbc[...] = jnp.zeros_like(hbc)

    for copy in load_x:
        copy.wait()

    def one_quad(i, _):
        q = lax.rem(plane // 2 + i, quads) if many else i
        at = pl.multiple_of(q * QW, QW)
        taps = [conv_x[lag : lag + 1, pl.ds(at, QW)] * 0.5 for lag in range(4)]
        pick = sel[:, pl.ds(at, QW)]

        def weighed_block(k):
            prev = hx[:, pl.ds(at, QW)] if k == 0 else xq[q, k * Q - HALO : k * Q, :]
            half = half_conv(xq[q, k * Q : (k + 1) * Q, :], prev, taps, keep[(k + 1) * Q - 8 : (k + 2) * Q, :])
            act = twice_silu_half(half)
            xc[q, k * Q : (k + 1) * Q, :] = act.astype(BF16)
            return (act * dot_t(whl[k], pick)).astype(BF16)

        def by_quad(ref, k):
            return jnp.concatenate([ref[k, pl.ds(2 * q, 1), :], ref[k, pl.ds(2 * q + 1, 1), :]], axis=1)

        held = dot(btr[1], weighed_block(1))
        for k in range(2, blocks):
            weighed = weighed_block(k)
            sk[q, k] = held.astype(BF16)
            held = held * by_quad(dec_blk, k) + dot(btr[k], weighed)

        @pl.when(i == 0)
        def _():
            if many:
                halo_x.wait()
                halo_bc.wait()
            btr[0] = conv_bc_block(0, 0).T.astype(BF16)

        block0 = dot(btr[0], weighed_block(0))
        fresh[q] = block0
        held = held + block0 * by_quad(dec_one, blocks)
        if many:
            for side in range(2):
                p = 2 * q + side
                for part in range(4):
                    owner = p * 4 + part
                    sbuf[p, part, :PART, :] = held[
                        part * PART : (part + 1) * PART, side * LANES : (side + 1) * LANES
                    ].astype(BF16)

                    @pl.when(owner != me)
                    def _():
                        pltpu.make_async_remote_copy(
                            src_ref=sbuf.at[p, part], dst_ref=got_s.at[me],
                            send_sem=sem_s.at[0], recv_sem=sem_r.at[0],
                            device_id={"ctx": owner}, device_id_type=MESH,
                        ).start()

                    @pl.when(owner == me)
                    def _():
                        got_s[me] = sbuf[p, part]

        return 0

    lax.fori_loop(0, quads, one_quad, 0)

    causal = iota((Q, Q), 0) >= iota((Q, Q), 1)
    for k in range(blocks):
        c_wide = conv_bc_block(k, LANES)
        c_mat = c_wide.astype(BF16)
        cwide[k * Q : (k + 1) * Q, :] = c_wide
        cmat[k * Q : (k + 1) * Q, :] = c_mat
        cb[k] = jnp.where(causal, dot(c_mat, btr[k]), 0.0).astype(BF16)
        cum = colf[k, :heads]
        ehl[k] = jnp.concatenate(two(jnp.exp2(cum)), axis=0)
        colf[k] = jnp.concatenate([cum, jnp.zeros((Q - heads, LANES), F32)], axis=0).T
        log_pre = by_pair(2 * k + 1)
        dec_pre[k] = jnp.exp2(log_pre)
        dec_one[k] = jnp.exp2(log_pre - one_on) if k else jnp.zeros_like(log_pre)
    for q in range(quads):
        sk[q, 0] = jnp.zeros((LANES, QW), BF16)
        sk[q, 1] = jnp.zeros((LANES, QW), BF16)

    for copy in load_z:
        copy.wait()
    left_bf = iota((Q, LANES), 1) < 64

    def one_block(k, _):
        rows = pl.ds(pl.multiple_of(k * Q, Q), Q)
        cb_k = cb[k]
        c_k = cmat[rows, :]
        for q in range(quads):
            out = []
            for side in range(2):
                pair = 2 * q + side
                weights = []
                for h in (2 * pair, 2 * pair + 1):
                    gap = colf[k, :, h : h + 1] + vrow[k, h : h + 1, :]
                    fade = jnp.where(causal, jnp.exp2(gap), 0.0).astype(BF16)
                    weights.append(fade * cb_k)
                x_pair = xc[q, rows, side * LANES : (side + 1) * LANES]
                zero = jnp.zeros_like(x_pair)
                both = jnp.concatenate([jnp.where(left_bf, x_pair, zero), jnp.where(left_bf, zero, x_pair)], axis=0)
                skip = jnp.where(iota((1, LANES), 1) < 64, d_skip[2 * pair], d_skip[2 * pair + 1])
                out.append(dot(jnp.concatenate(weights, axis=1), both) + skip * x_pair.astype(F32))
            fade_in = dot_t(ehl[k], sel[:, q * QW : (q + 1) * QW])
            since = jnp.concatenate([dec_one[k, 2 * q : 2 * q + 1, :], dec_one[k, 2 * q + 1 : 2 * q + 2, :]], axis=1)
            start = (sk[q, k].astype(F32) + since * fresh[q]).astype(BF16)
            inside = jnp.concatenate(out, axis=1) + fade_in * dot(c_k, start)
            gate = twice_silu_half(zq[q, rows, :].astype(F32) * 0.5)
            dec = jnp.concatenate([dec_pre[k, 2 * q : 2 * q + 1, :], dec_pre[k, 2 * q + 1 : 2 * q + 2, :]], axis=1)
            part_a[q, rows, :] = inside * gate
            part_b[q, rows, :] = fade_in * dec * gate
        return 0

    lax.fori_loop(0, split, one_block, 0)

    def all_of(sem, like, count):
        view = like.at[pl.ds(0, count)]
        pltpu.make_async_copy(view, view, sem).wait()

    if many:
        all_of(sem_r.at[0], got_s, n_ctx - 1)

        def lap(d, acc):
            ret_s[d] = acc.astype(BF16)
            dec = jnp.sum(got_s[d, PART:, :].astype(F32), axis=0, keepdims=True)
            return acc * dec + got_s[d, :PART, :].astype(F32)

        lax.fori_loop(0, n_ctx, lap, jnp.zeros((PART, LANES), F32), unroll=True)

        def send_back(i, _):
            other = lax.rem(me + i, n_ctx)
            pltpu.make_async_remote_copy(
                src_ref=ret_s.at[other], dst_ref=inbound.at[plane, lane_y],
                send_sem=sem_s.at[1], recv_sem=sem_r.at[1],
                device_id={"ctx": other}, device_id_type=MESH,
            ).start()
            return 0

        lax.fori_loop(1, n_ctx, send_back, 0)
        inbound[plane, lane_y] = ret_s[me]

    lax.fori_loop(split, blocks, one_block, 0)

    for c, end in enumerate(ends):
        spot = end - me * rows_all
        mine = jnp.where((spot >= 0) & (spot < rows_all), 1.0, 0.0)
        spot = jnp.minimum(jnp.maximum(spot, 0), rows_all - 1)
        end_c[c : c + 1, :] = cwide[pl.ds(spot, 1), :]
        for q in range(quads):
            end_a[c : c + 1, q * QW : (q + 1) * QW] = part_a[q, pl.ds(spot, 1), :] * mine
            end_b[c : c + 1, q * QW : (q + 1) * QW] = part_b[q, pl.ds(spot, 1), :] * mine

    if many:
        all_of(sem_r.at[1], ret_s, n_ctx - 1)
    else:
        inbound[...] = jnp.zeros_like(inbound)
    for p in range(pairs):
        sin[:, p * LANES : (p + 1) * LANES] = inbound[p].reshape(LANES, LANES)

    last = end_a[...] + end_b[...] * dot(end_c[...].astype(BF16), sin[...])
    width = heads * 64
    inv = lax.rsqrt(jnp.sum(last * last, axis=1, keepdims=True) * (1.0 / width) + 1e-05)
    rounded = (last * inv * gain[...].reshape(1, width)).astype(BF16).astype(F32)
    score = jnp.sum(rounded * readout[...].astype(F32).reshape(1, width), axis=1, keepdims=True)
    diag = iota((TABLE, LANES), 0) == iota((TABLE, LANES), 1)
    score_row = jnp.sum(jnp.where(diag, score, 0.0), axis=0, keepdims=True)
    if many:
        sc_mine[0] = score_row

        def to_head(i, _):
            pltpu.make_async_remote_copy(
                src_ref=sc_mine.at[0], dst_ref=got_h.at[me_head],
                send_sem=sem_s.at[2], recv_sem=sem_r.at[2],
                device_id={"head": lax.rem(me_head + i, n_head)}, device_id_type=MESH,
            ).start()
            return 0

        lax.fori_loop(1, n_head, to_head, 0)
        got_h[me_head] = score_row

    def finish(k, _):
        rows = pl.ds(pl.multiple_of(k * Q, Q), Q)
        c_k = cmat[rows, :]
        squares = jnp.zeros((Q, LANES), F32)
        for q in range(quads):
            value = part_a[q, rows, :] + part_b[q, rows, :] * dot(c_k, sin[:, q * QW : (q + 1) * QW])
            part_a[q, rows, :] = value
            square = value * value
            squares = squares + square[:, :LANES] + square[:, LANES:]
        inv = lax.rsqrt(jnp.sum(squares, axis=1, keepdims=True) * (1.0 / width) + 1e-05)
        gain_row = gain[...].reshape(1, width)
        for q in range(quads):
            mixed = part_a[q, rows, :] * inv * gain_row[:, q * QW : (q + 1) * QW]
            stage[rows, q * QW : (q + 1) * QW] = mixed.astype(BF16)
        pltpu.make_async_copy(stage.at[rows, :], out_hbm.at[rows, :], sem_out).start()
        return 0

    lax.fori_loop(0, blocks // 2, finish, 0)
    if many:
        all_of(sem_r.at[2], got_h, n_head - 1)
        score_row = jnp.sum(got_h[...], axis=0)
        sc_ctx[0] = score_row

        def to_ctx(i, _):
            pltpu.make_async_remote_copy(
                src_ref=sc_ctx.at[0], dst_ref=got_c.at[me],
                send_sem=sem_s.at[3], recv_sem=sem_r.at[3],
                device_id={"ctx": lax.rem(me + i, n_ctx)}, device_id_type=MESH,
            ).start()
            return 0

        lax.fori_loop(1, n_ctx, to_ctx, 0)
        got_c[me] = score_row
    lax.fori_loop(blocks // 2, blocks, finish, 0)
    if many:
        all_of(sem_s.at[0], got_s, n_ctx - 1)
        all_of(sem_s.at[1], ret_s, n_ctx - 1)
        all_of(sem_s.at[2], got_h, n_head - 1)
        all_of(sem_s.at[3], got_c, n_ctx - 1)
        all_of(sem_r.at[3], got_c, n_ctx - 1)
        score_row = jnp.sum(got_c[...], axis=0)
    score_ref[...] = score_row[0, : score_ref.shape[0]]
    pltpu.make_async_copy(stage, out_hbm, sem_out).wait()


def local(n_ctx, n_head, x_in, gate_z, bc_in, dt_raw, conv_x, conv_bc, dt_bias, a_log, d_skip, norm_gain, readout, lengths):
    rows, width = x_in.shape
    heads = dt_raw.shape[1]
    blocks, quads, pairs = rows // Q, width // QW, heads // 2
    vmem = pl.BlockSpec(memory_space=pltpu.VMEM)
    anywhere = pl.BlockSpec(memory_space=pl.ANY)
    hbm = pl.BlockSpec(memory_space=pltpu.HBM)
    dma = pltpu.SemaphoreType.DMA
    scratch = [
        pltpu.SMEM(lengths.shape, I32),
        pltpu.SMEM(dt_bias.shape, F32),
        pltpu.SMEM(a_log.shape, F32),
        pltpu.SMEM(d_skip.shape, F32),
        pltpu.VMEM((heads, rows), F32),
        pltpu.VMEM(conv_x.shape, F32),
        pltpu.VMEM(conv_bc.shape, F32),
        pltpu.VMEM(norm_gain.shape, F32),
        pltpu.VMEM(readout.shape, BF16),
        pltpu.VMEM((quads, rows, QW), BF16),
        pltpu.VMEM((rows, 256), BF16),
        pltpu.VMEM((quads, rows, QW), BF16),
        pltpu.VMEM((HALO, width), BF16),
        pltpu.VMEM((HALO, 256), BF16),
        pltpu.VMEM((rows + Q, LANES), F32),
        pltpu.VMEM((blocks, Q, Q), F32),
        pltpu.VMEM((blocks, heads, LANES), F32),
        pltpu.VMEM((blocks, 2 * heads, LANES), BF16),
        pltpu.VMEM((blocks, 2 * heads, LANES), BF16),
        pltpu.VMEM((2 * blocks + 1, heads, LANES), F32),
        pltpu.VMEM((blocks, pairs, LANES), F32),
        pltpu.VMEM((blocks, pairs, LANES), F32),
        pltpu.VMEM((2 * heads, width), BF16),
        pltpu.VMEM((quads, rows, QW), BF16),
        pltpu.VMEM((rows, LANES), BF16),
        pltpu.VMEM((rows, LANES), F32),
        pltpu.VMEM((blocks, LANES, Q), BF16),
        pltpu.VMEM((blocks, Q, Q), BF16),
        pltpu.VMEM((quads, blocks, LANES, QW), BF16),
        pltpu.VMEM((quads, LANES, QW), F32),
        pltpu.VMEM((blocks + 1, pairs, LANES), F32),
        pltpu.VMEM((pairs, 4, MSG, LANES), BF16),
        pltpu.VMEM((quads, rows, QW), F32),
        pltpu.VMEM((quads, rows, QW), F32),
        pltpu.VMEM((rows, width), BF16),
        pltpu.VMEM((LANES, width), BF16),
        pltpu.VMEM((TABLE, width), F32),
        pltpu.VMEM((TABLE, width), F32),
        pltpu.VMEM((TABLE, LANES), F32),
        pltpu.VMEM((n_ctx, MSG, LANES), BF16),
        pltpu.VMEM((n_ctx, PART, LANES), BF16),
        pltpu.VMEM((pairs, 4, PART, LANES), BF16),
        pltpu.VMEM((1, 1, LANES), F32),
        pltpu.VMEM((1, 1, LANES), F32),
        pltpu.VMEM((n_head, 1, LANES), F32),
        pltpu.VMEM((n_ctx, 1, LANES), F32),
        dma((9,)), dma((quads,)), dma, dma((quads,)), dma, dma((2,)), dma((2,)), dma((4,)), dma((4,)),
    ]
    params = dict(vmem_limit_bytes=50 * 1024 * 1024)
    if n_ctx > 1:
        params.update(collective_id=0, has_side_effects=True)
    split = min(3, blocks)
    return pl.pallas_call(
        functools.partial(kernel, (n_ctx, n_head, rows, heads, split)),
        out_shape=(jax.ShapeDtypeStruct((rows, width), BF16), jax.ShapeDtypeStruct(lengths.shape, F32)),
        in_specs=[hbm] * 12,
        out_specs=(anywhere, vmem),
        scratch_shapes=scratch,
        compiler_params=pltpu.CompilerParams(**params),
    )(
        *(
            pltpu.with_memory_space_constraint(array, pltpu.HBM)
            for array in (
                lengths, dt_bias, a_log, d_skip,
                dt_raw.T, conv_x, conv_bc, norm_gain, readout,
                x_in, gate_z, bc_in.reshape(rows, bc_in.shape[2]),
            )
        )
    )


def solution(mesh):
    in_specs = (
        P("ctx", "head"),
        P("ctx", "head"),
        P("ctx", "head", None),
        P("ctx", "head"),
        P(None, "head"),
        P(None, "head", None),
        P("head"),
        P("head"),
        P("head"),
        P("head"),
        P("head"),
        P(),
    )
    out_specs = (P("ctx", "head"), P())
    step = functools.partial(local, mesh.shape["ctx"], mesh.shape["head"])
    return jax.shard_map(step, mesh=mesh, in_specs=in_specs, out_specs=out_specs, check_vma=False)
```

```python
import functools

import jax
import jax.numpy as jnp
from jax import lax
from jax.experimental import pallas as pl
from jax.experimental.pallas import tpu as pltpu
from jax.sharding import PartitionSpec as P

F32, BF16, I32 = jnp.float32, jnp.bfloat16, jnp.int32
MESH = pl.DeviceIdType.MESH
LOG2E = 1.4426950408889634
Q = 128
QW = 256
HALO = 16
RESET = 200.0
LANES = 128
TABLE = 16
PART = 16
TILES = LANES // PART


def iota(shape, dim):
    return lax.broadcasted_iota(I32, shape, dim)


def dot(a, b):
    return jnp.dot(a, b, preferred_element_type=F32)


def dot_t(a, b):
    return lax.dot_general(a, b, (((0,), (0,)), ((), ())), preferred_element_type=F32)


def two(x):
    hi = x.astype(BF16)
    return hi, (x - hi.astype(F32)).astype(BF16)


def three(x):
    hi = x.astype(BF16)
    return (hi,) + two(x - hi.astype(F32))


def softplus(v):
    u = jnp.exp(-jnp.abs(v))
    small = u * (1.0 + u * (-0.5 + u * (1.0 / 3.0 - 0.25 * u)))
    return jnp.maximum(v, 0.0) + jnp.where(u < 0.01, small, jnp.log(1.0 + u))


def twice_silu_half(h):
    return h + h * jnp.tanh(h)


def half_conv(rows, before, taps, keep, buf, slot):
    outs = []
    tiles = rows.shape[1] // LANES
    x = jnp.concatenate([before.astype(F32)[HALO - 8 :], rows.astype(F32)], axis=0)
    for t in range(tiles):
        buf[2 * slot + t] = x[:, t * LANES : (t + 1) * LANES]
    for t in range(tiles):
        tap = [w[:, t * LANES : (t + 1) * LANES] for w in taps]
        late = [buf[2 * slot + t, 8 - lag : 8 - lag + Q, :] for lag in (1, 2, 3)]
        acc = late[2] * tap[3] * keep[2]
        acc = (acc + late[1] * tap[2]) * keep[1]
        acc = (acc + late[0] * tap[1]) * keep[0]
        outs.append(acc + x[8:, t * LANES : (t + 1) * LANES] * tap[0])
    return outs[0] if tiles == 1 else jnp.concatenate(outs, axis=1)


def kernel(
    dims,
    lengths_hbm, bias_hbm, a_log_hbm, d_skip_hbm,
    dt_hbm, conv_x_hbm, conv_bc_hbm, gain_hbm, readout_hbm, x_hbm, z_hbm, bc_hbm,
    out_hbm, score_ref,
    lengths, bias, a_log, d_skip, dt_ref, conv_x, conv_bc, gain, readout,
    xq, bcs, zq, hx, hbc, keep, keep2, keep3, buf, colf, vrow, whl, ehl, tots, dec_blk, dec_pre, sel,
    xc, cmat, cwide, btr, cb, sk, fresh, held_all, dec_one, sbuf, part_a, part_b, stage, sin, end_a, end_b, end_c,
    my_dec, got_dec, got_s, ret_s, inbound, sc_mine, sc_ctx, got_h, got_c,
    sem_small, sem_x, sem_bc, sem_z, sem_out, sem_halo_s, sem_halo_r, sem_a, sem_s, sem_r,
):
    n_ctx, n_head, rows_all, heads, split = dims
    blocks = rows_all // Q
    quads = heads * 64 // QW
    pairs = heads // 2
    many = n_ctx > 1
    me = lax.axis_index("ctx")
    me_head = lax.axis_index("head")
    my_side, my_tile = me // 16, lax.rem(me // 2, TILES)

    load_small = [
        pltpu.make_async_copy(source, target, sem_small.at[i])
        for i, (source, target) in enumerate(
            [
                (lengths_hbm, lengths), (bias_hbm, bias), (a_log_hbm, a_log), (d_skip_hbm, d_skip),
                (dt_hbm, dt_ref), (conv_x_hbm, conv_x), (conv_bc_hbm, conv_bc), (gain_hbm, gain), (readout_hbm, readout),
            ]
        )
    ]
    for copy in load_small:
        copy.start()
    load_bc = pltpu.make_async_copy(bc_hbm, bcs, sem_bc)
    load_bc.start()
    load_x = [
        pltpu.make_async_copy(x_hbm.at[:, pl.ds(q * QW, QW)], xq.at[q], sem_x.at[q])
        for q in range(quads)
    ]
    load_z = [
        pltpu.make_async_copy(z_hbm.at[:, pl.ds(q * QW, QW)], zq.at[q], sem_z.at[q])
        for q in range(quads)
    ]
    for copy in load_x + load_z:
        copy.start()

    if many:
        barrier = pltpu.get_barrier_semaphore()

        def greet_ctx(i, _):
            pl.semaphore_signal(barrier, inc=1, device_id={"ctx": lax.rem(me + i, n_ctx)}, device_id_type=MESH)
            return 0

        lax.fori_loop(1, n_ctx, greet_ctx, 0)

        def greet_head(i, _):
            pl.semaphore_signal(barrier, inc=1, device_id={"head": lax.rem(me_head + i, n_head)}, device_id_type=MESH)
            return 0

        lax.fori_loop(1, n_head, greet_head, 0)

    for copy in load_small:
        copy.wait()

    offset = jnp.int32(0)
    here = me * rows_all + (iota((TABLE, LANES), 0) - 1) * Q + iota((TABLE, LANES), 1)
    first = jnp.zeros((TABLE, LANES), F32)
    ends = []
    for c in range(lengths.shape[0]):
        first = jnp.where(here == offset, 1.0, first)
        offset = offset + lengths[c]
        ends.append(offset - 1)

    head_row = iota((heads, LANES), 0)
    bias_col = jnp.zeros((heads, LANES), F32)
    rate_col = jnp.zeros((heads, LANES), F32)
    for h in range(heads):
        bias_col = jnp.where(head_row == h, bias[h], bias_col)
        rate_col = jnp.where(head_row == h, a_log[h], rate_col)
    rate_col = jnp.exp(rate_col) * (-LOG2E)
    steps, logs = [], []
    for k in range(blocks):
        dt_vals = softplus(dt_ref[:, k * Q : (k + 1) * Q] + bias_col)
        steps.append(jnp.log(dt_vals) * LOG2E)
        logs.append(dt_vals * rate_col - RESET * first[k + 1 : k + 2])
    upper = (iota((Q, Q), 0) <= iota((Q, Q), 1)).astype(F32).astype(BF16)
    cum_all = dot(
        jnp.concatenate(three(jnp.concatenate(logs, axis=0)), axis=1),
        jnp.concatenate([upper] * 3, axis=0),
    )
    before = jnp.zeros((heads, LANES), F32)
    for k in range(blocks):
        cum = cum_all[k * heads : (k + 1) * heads]
        value = steps[k] - cum
        total = jnp.broadcast_to(cum[:, Q - 1 : Q], (heads, LANES))
        vrow[k] = value
        colf[k, :heads] = cum
        whl[k] = jnp.concatenate(two(jnp.exp2(total + value)), axis=0)
        tots[2 * k] = total
        tots[2 * k + 1] = before
        before = before + total
    tots[2 * blocks] = before
    left = iota((pairs, LANES), 1) < 64

    def by_pair(i):
        return jnp.where(left, tots[i, pl.ds(0, pairs, stride=2), :], tots[i, pl.ds(1, pairs, stride=2), :])

    one_on = by_pair(3)
    for k in range(blocks):
        dec_blk[k] = jnp.exp2(by_pair(2 * k))
    dec_one[blocks] = jnp.exp2(by_pair(2 * blocks) - one_on)

    sel_row, sel_head = iota((2 * heads, heads * 64), 0), iota((2 * heads, heads * 64), 1) // 64
    sel[...] = jnp.where((sel_row == sel_head) | (sel_row == sel_head + heads), 1.0, 0.0).astype(BF16)
    later = 1.0 - first
    shifted = []
    for lag in (1, 2):
        here_l = pltpu.roll(later, lag, 1)
        over = jnp.concatenate([here_l[:1], here_l[:-1]], axis=0)
        shifted.append(jnp.where(iota((TABLE, LANES), 1) < lag, over, here_l))
    stay2 = later * shifted[0]
    stay3 = stay2 * shifted[1]
    keep_col = jnp.concatenate([later, stay2, stay3, jnp.zeros((LANES - 3 * TABLE, LANES), F32)], axis=0).T
    for k in range(blocks):
        for j, m in enumerate((keep, keep2, keep3)):
            m[k * Q : (k + 1) * Q, :] = jnp.broadcast_to(keep_col[:, j * TABLE + k + 1 : j * TABLE + k + 2], (Q, LANES))

    load_bc.wait()
    bc_taps = [conv_bc[lag] * 0.5 for lag in range(4)]

    def conv_bc_block(k, at):
        prev = hbc[:, at : at + LANES] if k == 0 else bcs[k * Q - HALO : k * Q, at : at + LANES]
        half = half_conv(
            bcs[k * Q : (k + 1) * Q, at : at + LANES], prev,
            [tap[:, at : at + LANES] for tap in bc_taps], [m[k * Q : (k + 1) * Q, :] for m in (keep, keep2, keep3)], buf, k % 6,
        )
        return twice_silu_half(half)

    for k in range(1, blocks):
        btr[k] = conv_bc_block(k, 0).T.astype(BF16)

    nxt = lax.rem(me + 1, n_ctx)
    if many:
        pl.semaphore_wait(barrier, n_ctx - 1 + n_head - 1)
        halo_x = pltpu.make_async_remote_copy(
            src_ref=x_hbm.at[pl.ds(rows_all - HALO, HALO), :], dst_ref=hx,
            send_sem=sem_halo_s.at[0], recv_sem=sem_halo_r.at[0],
            device_id={"ctx": nxt}, device_id_type=MESH,
        )
        halo_bc = pltpu.make_async_remote_copy(
            src_ref=bc_hbm.at[pl.ds(rows_all - HALO, HALO), :], dst_ref=hbc,
            send_sem=sem_halo_s.at[1], recv_sem=sem_halo_r.at[1],
            device_id={"ctx": nxt}, device_id_type=MESH,
        )
        halo_x.start()
        halo_bc.start()
        dec_all = jnp.exp2(by_pair(2 * blocks))
        for p in range(4):
            my_dec[p] = jnp.concatenate([dec_all[p : p + 1], dec_all[p + 4 : p + 5]], axis=0)

        def send_dec(i, _):
            other = lax.rem(me + i, n_ctx)
            pltpu.make_async_remote_copy(
                src_ref=my_dec.at[2 * lax.rem(other, 2) + other // 16], dst_ref=got_dec.at[me],
                send_sem=sem_s.at[4], recv_sem=sem_r.at[4],
                device_id={"ctx": other}, device_id_type=MESH,
            ).start()
            return 0

        lax.fori_loop(1, n_ctx, send_dec, 0)
        got_dec[me] = my_dec[2 * lax.rem(me, 2) + my_side]
    else:
        hx[...] = jnp.zeros_like(hx)
        hbc[...] = jnp.zeros_like(hbc)

    for copy in load_x:
        copy.wait()

    def quad_of(i):
        at = pl.multiple_of(i * QW, QW)
        return i, at, [conv_x[lag : lag + 1, pl.ds(at, QW)] * 0.5 for lag in range(4)]

    def weighed_block(quad, k):
        q, at, taps = quad
        prev = hx[:, pl.ds(at, QW)] if k == 0 else xq[q, k * Q - HALO : k * Q, :]
        half = half_conv(xq[q, k * Q : (k + 1) * Q, :], prev, taps, [m[k * Q : (k + 1) * Q, :] for m in (keep, keep2, keep3)], buf, k % 6)
        act = twice_silu_half(half)
        xc[q, k * Q : (k + 1) * Q, :] = act.astype(BF16)
        return (act * dot_t(whl[k], sel[:, pl.ds(at, QW)])).astype(BF16)

    def by_quad(ref, k, q):
        return jnp.concatenate([ref[k, pl.ds(2 * q, 1), :], ref[k, pl.ds(2 * q + 1, 1), :]], axis=1)

    def first_block(i, _):
        quad = quad_of(i)
        q = quad[0]
        block0 = dot(btr[0], weighed_block(quad, 0))
        fresh[q] = block0
        held = held_all[q] + block0 * by_quad(dec_one, blocks, q)
        if many:
            for u in range(2 * TILES):
                side, tile = u // TILES, u % TILES
                sbuf[q * 2 * TILES + u] = held[
                    tile * PART : (tile + 1) * PART, side * LANES : (side + 1) * LANES
                ].astype(BF16)
            slot = q // 2

            def send_state(u, _):
                owner = 2 * u + lax.rem(q, 2)

                @pl.when(owner != me)
                def _():
                    pltpu.make_async_remote_copy(
                        src_ref=sbuf.at[q * 2 * TILES + u], dst_ref=got_s.at[slot * n_ctx + me],
                        send_sem=sem_s.at[0], recv_sem=sem_a.at[slot],
                        device_id={"ctx": owner}, device_id_type=MESH,
                    ).start()

                @pl.when(owner == me)
                def _():
                    got_s[slot * n_ctx + me] = sbuf[q * 2 * TILES + u]

                return 0

            lax.fori_loop(0, 2 * TILES, send_state, 0)
        return 0

    def one_quad(i, _):
        quad = quad_of(i)
        q = quad[0]
        held = dot(btr[1], weighed_block(quad, 1))
        for k in range(2, blocks):
            weighed = weighed_block(quad, k)
            sk[q, k] = held.astype(BF16)
            held = held * by_quad(dec_blk, k, q) + dot(btr[k], weighed)
        held_all[q] = held

        @pl.when(i == 1)
        def _():
            if many:
                halo_x.wait()
                halo_bc.wait()
            btr[0] = conv_bc_block(0, 0).T.astype(BF16)

        lax.fori_loop(jnp.where(i == 1, 0, i), jnp.where(i == 0, 0, i + 1), first_block, 0)
        return 0

    lax.fori_loop(0, quads, one_quad, 0)

    def all_of(sem, like, count):
        view = like.at[pl.ds(0, count)]
        pltpu.make_async_copy(view, view, sem).wait()

    def scan_part(slot):
        all_of(sem_a.at[slot], got_s, n_ctx - 1)
        base = slot * n_ctx

        def lap(d, acc):
            ret_s[base + d] = acc.astype(BF16)
            return acc * got_dec[d, slot : slot + 1, :] + got_s[base + d].astype(F32)

        lax.fori_loop(0, n_ctx, lap, jnp.zeros((PART, LANES), F32), unroll=True)
        target = (4 * slot + 2 * lax.rem(me, 2) + my_side) * TILES + my_tile

        def send_back(i, _):
            d = lax.rem(me + i, n_ctx)
            pltpu.make_async_remote_copy(
                src_ref=ret_s.at[base + d], dst_ref=inbound.at[target],
                send_sem=sem_s.at[1], recv_sem=sem_r.at[1],
                device_id={"ctx": d}, device_id_type=MESH,
            ).start()
            return 0

        lax.fori_loop(1, n_ctx, send_back, 0)
        inbound[target] = ret_s[base + me]

    if many:
        all_of(sem_r.at[4], got_dec, n_ctx - 1)
        scan_part(0)

    causal = iota((Q, Q), 0) >= iota((Q, Q), 1)
    for k in range(blocks):
        c_wide = conv_bc_block(k, LANES)
        c_mat = c_wide.astype(BF16)
        cwide[k * Q : (k + 1) * Q, :] = c_wide
        cmat[k * Q : (k + 1) * Q, :] = c_mat
        cb[k] = jnp.where(causal, dot(c_mat, btr[k]), 0.0).astype(BF16)
        cum = colf[k, :heads]
        ehl[k] = jnp.concatenate(two(jnp.exp2(cum)), axis=0)
        colf[k] = jnp.concatenate([cum, jnp.zeros((Q - heads, LANES), F32)], axis=0).T
        log_pre = by_pair(2 * k + 1)
        dec_pre[k] = jnp.exp2(log_pre)
        dec_one[k] = jnp.exp2(log_pre - one_on) if k else jnp.zeros_like(log_pre)
    for q in range(quads):
        sk[q, 0] = jnp.zeros((LANES, QW), BF16)
        sk[q, 1] = jnp.zeros((LANES, QW), BF16)

    for copy in load_z:
        copy.wait()
    left_bf = iota((Q, LANES), 1) < 64

    def one_block(k, _):
        rows = pl.ds(pl.multiple_of(k * Q, Q), Q)
        cb_k = cb[k]
        c_k = cmat[rows, :]
        for q in range(quads):
            out = []
            for side in range(2):
                pair = 2 * q + side
                weights = []
                for h in (2 * pair, 2 * pair + 1):
                    gap = colf[k, :, h : h + 1] + vrow[k, h : h + 1, :]
                    fade = jnp.where(causal, jnp.exp2(gap), 0.0).astype(BF16)
                    weights.append(fade * cb_k)
                x_pair = xc[q, rows, side * LANES : (side + 1) * LANES]
                zero = jnp.zeros_like(x_pair)
                both = jnp.concatenate([jnp.where(left_bf, x_pair, zero), jnp.where(left_bf, zero, x_pair)], axis=0)
                skip = jnp.where(iota((1, LANES), 1) < 64, d_skip[2 * pair], d_skip[2 * pair + 1])
                out.append(dot(jnp.concatenate(weights, axis=1), both) + skip * x_pair.astype(F32))
            fade_in = dot_t(ehl[k], sel[:, q * QW : (q + 1) * QW])
            since = jnp.concatenate([dec_one[k, 2 * q : 2 * q + 1, :], dec_one[k, 2 * q + 1 : 2 * q + 2, :]], axis=1)
            start = (sk[q, k].astype(F32) + since * fresh[q]).astype(BF16)
            inside = jnp.concatenate(out, axis=1) + fade_in * dot(c_k, start)
            gate = twice_silu_half(zq[q, rows, :].astype(F32) * 0.5)
            dec = jnp.concatenate([dec_pre[k, 2 * q : 2 * q + 1, :], dec_pre[k, 2 * q + 1 : 2 * q + 2, :]], axis=1)
            part_a[q, rows, :] = inside * gate
            part_b[q, rows, :] = fade_in * dec * gate
        return 0

    lax.fori_loop(0, split, one_block, 0)

    if many:
        scan_part(1)

    lax.fori_loop(split, blocks, one_block, 0)

    for c, end in enumerate(ends):
        spot = end - me * rows_all
        mine = jnp.where((spot >= 0) & (spot < rows_all), 1.0, 0.0)
        spot = jnp.minimum(jnp.maximum(spot, 0), rows_all - 1)
        end_c[c : c + 1, :] = cwide[pl.ds(spot, 1), :]
        for q in range(quads):
            end_a[c : c + 1, q * QW : (q + 1) * QW] = part_a[q, pl.ds(spot, 1), :] * mine
            end_b[c : c + 1, q * QW : (q + 1) * QW] = part_b[q, pl.ds(spot, 1), :] * mine

    if many:
        all_of(sem_r.at[1], inbound, 2 * n_ctx - 2)
    else:
        inbound[...] = jnp.zeros_like(inbound)
    for p in range(pairs):
        sin[:, p * LANES : (p + 1) * LANES] = inbound[p * TILES : (p + 1) * TILES].reshape(LANES, LANES)

    last = end_a[...] + end_b[...] * dot(end_c[...].astype(BF16), sin[...])
    width = heads * 64
    inv = lax.rsqrt(jnp.sum(last * last, axis=1, keepdims=True) * (1.0 / width) + 1e-05)
    rounded = (last * inv * gain[...].reshape(1, width)).astype(BF16).astype(F32)
    score = jnp.sum(rounded * readout[...].astype(F32).reshape(1, width), axis=1, keepdims=True)
    diag = iota((TABLE, LANES), 0) == iota((TABLE, LANES), 1)
    score_row = jnp.sum(jnp.where(diag, score, 0.0), axis=0, keepdims=True)
    if many:
        sc_mine[0] = score_row

        def to_head(i, _):
            pltpu.make_async_remote_copy(
                src_ref=sc_mine.at[0], dst_ref=got_h.at[me_head],
                send_sem=sem_s.at[2], recv_sem=sem_r.at[2],
                device_id={"head": lax.rem(me_head + i, n_head)}, device_id_type=MESH,
            ).start()
            return 0

        lax.fori_loop(1, n_head, to_head, 0)
        got_h[me_head] = score_row

    def finish(k, _):
        rows = pl.ds(pl.multiple_of(k * Q, Q), Q)
        c_k = cmat[rows, :]
        squares = jnp.zeros((Q, LANES), F32)
        for q in range(quads):
            value = part_a[q, rows, :] + part_b[q, rows, :] * dot(c_k, sin[:, q * QW : (q + 1) * QW])
            part_a[q, rows, :] = value
            square = value * value
            squares = squares + square[:, :LANES] + square[:, LANES:]
        inv = lax.rsqrt(jnp.sum(squares, axis=1, keepdims=True) * (1.0 / width) + 1e-05)
        gain_row = gain[...].reshape(1, width)
        for q in range(quads):
            mixed = part_a[q, rows, :] * inv * gain_row[:, q * QW : (q + 1) * QW]
            stage[rows, q * QW : (q + 1) * QW] = mixed.astype(BF16)
        pltpu.make_async_copy(stage.at[rows, :], out_hbm.at[rows, :], sem_out).start()
        return 0

    lax.fori_loop(0, blocks // 2, finish, 0)
    if many:
        all_of(sem_r.at[2], got_h, n_head - 1)
        score_row = jnp.sum(got_h[...], axis=0)
        sc_ctx[0] = score_row

        def to_ctx(i, _):
            pltpu.make_async_remote_copy(
                src_ref=sc_ctx.at[0], dst_ref=got_c.at[me],
                send_sem=sem_s.at[3], recv_sem=sem_r.at[3],
                device_id={"ctx": lax.rem(me + i, n_ctx)}, device_id_type=MESH,
            ).start()
            return 0

        lax.fori_loop(1, n_ctx, to_ctx, 0)
        got_c[me] = score_row
    lax.fori_loop(blocks // 2, blocks, finish, 0)
    if many:
        all_of(sem_s.at[0], got_s, 2 * n_ctx - 2)
        all_of(sem_s.at[1], ret_s, 2 * n_ctx - 2)
        all_of(sem_s.at[2], got_h, n_head - 1)
        all_of(sem_s.at[3], got_c, n_ctx - 1)
        all_of(sem_s.at[4], got_dec, n_ctx - 1)
        all_of(sem_r.at[3], got_c, n_ctx - 1)
        score_row = jnp.sum(got_c[...], axis=0)
    score_ref[...] = score_row[0, : score_ref.shape[0]]
    pltpu.make_async_copy(stage, out_hbm, sem_out).wait()


def local(n_ctx, n_head, x_in, gate_z, bc_in, dt_raw, conv_x, conv_bc, dt_bias, a_log, d_skip, norm_gain, readout, lengths):
    rows, width = x_in.shape
    heads = dt_raw.shape[1]
    blocks, quads, pairs = rows // Q, width // QW, heads // 2
    vmem = pl.BlockSpec(memory_space=pltpu.VMEM)
    anywhere = pl.BlockSpec(memory_space=pl.ANY)
    hbm = pl.BlockSpec(memory_space=pltpu.HBM)
    dma = pltpu.SemaphoreType.DMA
    scratch = [
        pltpu.SMEM(lengths.shape, I32),
        pltpu.SMEM(dt_bias.shape, F32),
        pltpu.SMEM(a_log.shape, F32),
        pltpu.SMEM(d_skip.shape, F32),
        pltpu.VMEM((heads, rows), F32),
        pltpu.VMEM(conv_x.shape, F32),
        pltpu.VMEM(conv_bc.shape, F32),
        pltpu.VMEM(norm_gain.shape, F32),
        pltpu.VMEM(readout.shape, BF16),
        pltpu.VMEM((quads, rows, QW), BF16),
        pltpu.VMEM((rows, 256), BF16),
        pltpu.VMEM((quads, rows, QW), BF16),
        pltpu.VMEM((HALO, width), BF16),
        pltpu.VMEM((HALO, 256), BF16),
        pltpu.VMEM((rows, LANES), F32),
        pltpu.VMEM((rows, LANES), F32),
        pltpu.VMEM((rows, LANES), F32),
        pltpu.VMEM((12, Q + 8, LANES), F32),
        pltpu.VMEM((blocks, Q, Q), F32),
        pltpu.VMEM((blocks, heads, LANES), F32),
        pltpu.VMEM((blocks, 2 * heads, LANES), BF16),
        pltpu.VMEM((blocks, 2 * heads, LANES), BF16),
        pltpu.VMEM((2 * blocks + 1, heads, LANES), F32),
        pltpu.VMEM((blocks, pairs, LANES), F32),
        pltpu.VMEM((blocks, pairs, LANES), F32),
        pltpu.VMEM((2 * heads, width), BF16),
        pltpu.VMEM((quads, rows, QW), BF16),
        pltpu.VMEM((rows, LANES), BF16),
        pltpu.VMEM((rows, LANES), F32),
        pltpu.VMEM((blocks, LANES, Q), BF16),
        pltpu.VMEM((blocks, Q, Q), BF16),
        pltpu.VMEM((quads, blocks, LANES, QW), BF16),
        pltpu.VMEM((quads, LANES, QW), F32),
        pltpu.VMEM((quads, LANES, QW), F32),
        pltpu.VMEM((blocks + 1, pairs, LANES), F32),
        pltpu.VMEM((pairs * LANES // PART, PART, LANES), BF16),
        pltpu.VMEM((quads, rows, QW), F32),
        pltpu.VMEM((quads, rows, QW), F32),
        pltpu.VMEM((rows, width), BF16),
        pltpu.VMEM((LANES, width), BF16),
        pltpu.VMEM((TABLE, width), F32),
        pltpu.VMEM((TABLE, width), F32),
        pltpu.VMEM((TABLE, LANES), F32),
        pltpu.VMEM((4, 2, LANES), F32),
        pltpu.VMEM((n_ctx, 2, LANES), F32),
        pltpu.VMEM((2 * n_ctx, PART, LANES), BF16),
        pltpu.VMEM((2 * n_ctx, PART, LANES), BF16),
        pltpu.VMEM((pairs * LANES // PART, PART, LANES), BF16),
        pltpu.VMEM((1, 1, LANES), F32),
        pltpu.VMEM((1, 1, LANES), F32),
        pltpu.VMEM((n_head, 1, LANES), F32),
        pltpu.VMEM((n_ctx, 1, LANES), F32),
        dma((9,)), dma((quads,)), dma, dma((quads,)), dma, dma((2,)), dma((2,)), dma((2,)), dma((5,)), dma((5,)),
    ]
    params = dict(vmem_limit_bytes=50 * 1024 * 1024)
    if n_ctx > 1:
        params.update(collective_id=0, has_side_effects=True)
    split = min(3, blocks)
    return pl.pallas_call(
        functools.partial(kernel, (n_ctx, n_head, rows, heads, split)),
        out_shape=(jax.ShapeDtypeStruct((rows, width), BF16), jax.ShapeDtypeStruct(lengths.shape, F32)),
        in_specs=[hbm] * 12,
        out_specs=(anywhere, vmem),
        scratch_shapes=scratch,
        compiler_params=pltpu.CompilerParams(**params),
    )(
        *(
            pltpu.with_memory_space_constraint(array, pltpu.HBM)
            for array in (
                lengths, dt_bias, a_log, d_skip,
                dt_raw.T, conv_x, conv_bc, norm_gain, readout,
                x_in, gate_z, bc_in.reshape(rows, bc_in.shape[2]),
            )
        )
    )


def solution(mesh):
    in_specs = (
        P("ctx", "head"),
        P("ctx", "head"),
        P("ctx", "head", None),
        P("ctx", "head"),
        P(None, "head"),
        P(None, "head", None),
        P("head"),
        P("head"),
        P("head"),
        P("head"),
        P("head"),
        P(),
    )
    out_specs = (P("ctx", "head"), P())
    step = functools.partial(local, mesh.shape["ctx"], mesh.shape["head"])
    return jax.shard_map(step, mesh=mesh, in_specs=in_specs, out_specs=out_specs, check_vma=False)
```

```python
import functools

import jax
import jax.numpy as jnp
from jax import lax
from jax.experimental import pallas as pl
from jax.experimental.pallas import tpu as pltpu
from jax.sharding import PartitionSpec as P

F32, BF16, I32 = jnp.float32, jnp.bfloat16, jnp.int32
MESH = pl.DeviceIdType.MESH
LOG2E = 1.4426950408889634
Q = 128
QW = 256
HALO = 16
RESET = 200.0
LANES = 128
TABLE = 16
PART = 16
TILES = LANES // PART


def iota(shape, dim):
    return lax.broadcasted_iota(I32, shape, dim)


def dot(a, b):
    return jnp.dot(a, b, preferred_element_type=F32)


def dot_t(a, b):
    return lax.dot_general(a, b, (((0,), (0,)), ((), ())), preferred_element_type=F32)


def two(x):
    hi = x.astype(BF16)
    return hi, (x - hi.astype(F32)).astype(BF16)


def three(x):
    hi = x.astype(BF16)
    return (hi,) + two(x - hi.astype(F32))


def softplus(v):
    u = jnp.exp(-jnp.abs(v))
    small = u * (1.0 + u * (-0.5 + u * (1.0 / 3.0 - 0.25 * u)))
    return jnp.maximum(v, 0.0) + jnp.where(u < 0.01, small, jnp.log(1.0 + u))


def twice_silu_half(h):
    return h + h * jnp.tanh(h)


def half_conv(rows, before, taps, keep, buf, slot):
    outs = []
    tiles = rows.shape[1] // LANES
    x = jnp.concatenate([before.astype(F32)[HALO - 8 :], rows.astype(F32)], axis=0)
    for t in range(tiles):
        buf[2 * slot + t] = x[:, t * LANES : (t + 1) * LANES]
    for t in range(tiles):
        tap = [w[:, t * LANES : (t + 1) * LANES] for w in taps]
        late = [buf[2 * slot + t, 8 - lag : 8 - lag + Q, :] for lag in (1, 2, 3)]
        acc = late[2] * tap[3] * keep[2]
        acc = (acc + late[1] * tap[2]) * keep[1]
        acc = (acc + late[0] * tap[1]) * keep[0]
        outs.append(acc + x[8:, t * LANES : (t + 1) * LANES] * tap[0])
    return outs[0] if tiles == 1 else jnp.concatenate(outs, axis=1)


def kernel(
    dims,
    lengths_hbm, bias_hbm, a_log_hbm, d_skip_hbm,
    dt_hbm, conv_x_hbm, conv_bc_hbm, gain_hbm, readout_hbm, x_hbm, z_hbm, bc_hbm,
    out_hbm, score_ref,
    lengths, bias, a_log, d_skip, dt_ref, conv_x, conv_bc, gain, readout,
    xq, bcs, zq, hx, hbc, keep, keep2, keep3, buf, colf, vrow, whl, ehl, tots, dec_blk, dec_pre, sel,
    xc, cmat, cwide, btr, cb, sk, fresh, held_all, dec_one, sbuf, part_a, part_b, stage, sin, end_a, end_b, end_c,
    my_dec, got_dec, got_s, ret_s, inbound, sc_mine, sc_ctx, got_h, got_c,
    sem_small, sem_x, sem_bc, sem_z, sem_out, sem_halo_s, sem_halo_r, sem_a, sem_s, sem_r,
):
    n_ctx, n_head, rows_all, heads, split = dims
    blocks = rows_all // Q
    quads = heads * 64 // QW
    pairs = heads // 2
    many = n_ctx > 1
    me = lax.axis_index("ctx")
    me_head = lax.axis_index("head")
    my_side, my_tile = me // 16, lax.rem(me // 2, TILES)

    load_small = [
        pltpu.make_async_copy(source, target, sem_small.at[i])
        for i, (source, target) in enumerate(
            [
                (lengths_hbm, lengths), (bias_hbm, bias), (a_log_hbm, a_log), (d_skip_hbm, d_skip),
                (dt_hbm, dt_ref), (conv_x_hbm, conv_x), (conv_bc_hbm, conv_bc), (gain_hbm, gain), (readout_hbm, readout),
            ]
        )
    ]
    for copy in load_small:
        copy.start()
    load_bc = pltpu.make_async_copy(bc_hbm, bcs, sem_bc)
    load_bc.start()
    load_x = [
        pltpu.make_async_copy(x_hbm.at[:, pl.ds(q * QW, QW)], xq.at[q], sem_x.at[q])
        for q in range(quads)
    ]
    load_z = [
        pltpu.make_async_copy(z_hbm.at[:, pl.ds(q * QW, QW)], zq.at[q], sem_z.at[q])
        for q in range(quads)
    ]
    for copy in load_x + load_z:
        copy.start()

    if many:
        barrier = pltpu.get_barrier_semaphore()

        def greet_ctx(i, _):
            pl.semaphore_signal(barrier, inc=1, device_id={"ctx": lax.rem(me + i, n_ctx)}, device_id_type=MESH)
            return 0

        lax.fori_loop(1, n_ctx, greet_ctx, 0)

        def greet_head(i, _):
            pl.semaphore_signal(barrier, inc=1, device_id={"head": lax.rem(me_head + i, n_head)}, device_id_type=MESH)
            return 0

        lax.fori_loop(1, n_head, greet_head, 0)

    for copy in load_small:
        copy.wait()

    offset = jnp.int32(0)
    here = me * rows_all + (iota((TABLE, LANES), 0) - 1) * Q + iota((TABLE, LANES), 1)
    first = jnp.zeros((TABLE, LANES), F32)
    ends = []
    for c in range(lengths.shape[0]):
        first = jnp.where(here == offset, 1.0, first)
        offset = offset + lengths[c]
        ends.append(offset - 1)

    head_row = iota((heads, LANES), 0)
    bias_col = jnp.zeros((heads, LANES), F32)
    rate_col = jnp.zeros((heads, LANES), F32)
    for h in range(heads):
        bias_col = jnp.where(head_row == h, bias[h], bias_col)
        rate_col = jnp.where(head_row == h, a_log[h], rate_col)
    rate_col = jnp.exp(rate_col) * (-LOG2E)
    steps, logs = [], []
    for k in range(blocks):
        dt_vals = softplus(dt_ref[:, k * Q : (k + 1) * Q] + bias_col)
        steps.append(jnp.log(dt_vals) * LOG2E)
        logs.append(dt_vals * rate_col - RESET * first[k + 1 : k + 2])
    upper = (iota((Q, Q), 0) <= iota((Q, Q), 1)).astype(F32).astype(BF16)
    cum_all = dot(
        jnp.concatenate(three(jnp.concatenate(logs, axis=0)), axis=1),
        jnp.concatenate([upper] * 3, axis=0),
    )
    before = jnp.zeros((heads, LANES), F32)
    for k in range(blocks):
        cum = cum_all[k * heads : (k + 1) * heads]
        value = steps[k] - cum
        total = jnp.broadcast_to(cum[:, Q - 1 : Q], (heads, LANES))
        vrow[k] = value
        colf[k, :heads] = cum
        whl[k] = jnp.concatenate(two(jnp.exp2(total + value)), axis=0)
        tots[2 * k] = total
        tots[2 * k + 1] = before
        before = before + total
    tots[2 * blocks] = before
    left = iota((pairs, LANES), 1) < 64

    def by_pair(i):
        return jnp.where(left, tots[i, pl.ds(0, pairs, stride=2), :], tots[i, pl.ds(1, pairs, stride=2), :])

    one_on = by_pair(3)
    for k in range(blocks):
        dec_blk[k] = jnp.exp2(by_pair(2 * k))
    dec_one[blocks] = jnp.exp2(by_pair(2 * blocks) - one_on)

    sel_row, sel_head = iota((2 * heads, heads * 64), 0), iota((2 * heads, heads * 64), 1) // 64
    sel[...] = jnp.where((sel_row == sel_head) | (sel_row == sel_head + heads), 1.0, 0.0).astype(BF16)
    later = 1.0 - first
    shifted = []
    for lag in (1, 2):
        here_l = pltpu.roll(later, lag, 1)
        over = jnp.concatenate([here_l[:1], here_l[:-1]], axis=0)
        shifted.append(jnp.where(iota((TABLE, LANES), 1) < lag, over, here_l))
    stay2 = later * shifted[0]
    stay3 = stay2 * shifted[1]
    keep_col = jnp.concatenate([later, stay2, stay3, jnp.zeros((LANES - 3 * TABLE, LANES), F32)], axis=0).T
    for k in range(blocks):
        for j, m in enumerate((keep, keep2, keep3)):
            m[k * Q : (k + 1) * Q, :] = jnp.broadcast_to(keep_col[:, j * TABLE + k + 1 : j * TABLE + k + 2], (Q, LANES))

    load_bc.wait()
    bc_taps = [conv_bc[lag] * 0.5 for lag in range(4)]

    def conv_bc_block(k, at):
        prev = hbc[:, at : at + LANES] if k == 0 else bcs[k * Q - HALO : k * Q, at : at + LANES]
        half = half_conv(
            bcs[k * Q : (k + 1) * Q, at : at + LANES], prev,
            [tap[:, at : at + LANES] for tap in bc_taps], [m[k * Q : (k + 1) * Q, :] for m in (keep, keep2, keep3)], buf, k % 6,
        )
        return twice_silu_half(half)

    for k in range(1, blocks):
        btr[k] = conv_bc_block(k, 0).T.astype(BF16)

    nxt = lax.rem(me + 1, n_ctx)
    if many:
        pl.semaphore_wait(barrier, n_ctx - 1 + n_head - 1)
        halo_x = pltpu.make_async_remote_copy(
            src_ref=x_hbm.at[pl.ds(rows_all - HALO, HALO), :], dst_ref=hx,
            send_sem=sem_halo_s.at[0], recv_sem=sem_halo_r.at[0],
            device_id={"ctx": nxt}, device_id_type=MESH,
        )
        halo_bc = pltpu.make_async_remote_copy(
            src_ref=bc_hbm.at[pl.ds(rows_all - HALO, HALO), :], dst_ref=hbc,
            send_sem=sem_halo_s.at[1], recv_sem=sem_halo_r.at[1],
            device_id={"ctx": nxt}, device_id_type=MESH,
        )
        halo_x.start()
        halo_bc.start()
        dec_all = jnp.exp2(by_pair(2 * blocks))
        for p in range(4):
            my_dec[p] = jnp.concatenate([dec_all[p : p + 1], dec_all[p + 4 : p + 5]], axis=0)

        def send_dec(i, _):
            other = lax.rem(me + i, n_ctx)
            pltpu.make_async_remote_copy(
                src_ref=my_dec.at[2 * lax.rem(other, 2) + other // 16], dst_ref=got_dec.at[me],
                send_sem=sem_s.at[4], recv_sem=sem_r.at[4],
                device_id={"ctx": other}, device_id_type=MESH,
            ).start()
            return 0

        lax.fori_loop(1, n_ctx, send_dec, 0, unroll=True)
        got_dec[me] = my_dec[2 * lax.rem(me, 2) + my_side]
    else:
        hx[...] = jnp.zeros_like(hx)
        hbc[...] = jnp.zeros_like(hbc)

    for copy in load_x:
        copy.wait()

    def quad_of(i):
        at = pl.multiple_of(i * QW, QW)
        return i, at, [conv_x[lag : lag + 1, pl.ds(at, QW)] * 0.5 for lag in range(4)]

    def weighed_block(quad, k):
        q, at, taps = quad
        prev = hx[:, pl.ds(at, QW)] if k == 0 else xq[q, k * Q - HALO : k * Q, :]
        half = half_conv(xq[q, k * Q : (k + 1) * Q, :], prev, taps, [m[k * Q : (k + 1) * Q, :] for m in (keep, keep2, keep3)], buf, k % 6)
        act = twice_silu_half(half)
        xc[q, k * Q : (k + 1) * Q, :] = act.astype(BF16)
        return (act * dot_t(whl[k], sel[:, pl.ds(at, QW)])).astype(BF16)

    def by_quad(ref, k, q):
        return jnp.concatenate([ref[k, pl.ds(2 * q, 1), :], ref[k, pl.ds(2 * q + 1, 1), :]], axis=1)

    def first_block(i, _):
        quad = quad_of(i)
        q = quad[0]
        block0 = dot(btr[0], weighed_block(quad, 0))
        fresh[q] = block0
        held = held_all[q] + block0 * by_quad(dec_one, blocks, q)
        if many:
            for u in range(2 * TILES):
                side, tile = u // TILES, u % TILES
                sbuf[q * 2 * TILES + u] = held[
                    tile * PART : (tile + 1) * PART, side * LANES : (side + 1) * LANES
                ].astype(BF16)
            slot = q // 2

            def send_state(u, _):
                owner = 2 * u + lax.rem(q, 2)

                @pl.when(owner != me)
                def _():
                    pltpu.make_async_remote_copy(
                        src_ref=sbuf.at[q * 2 * TILES + u], dst_ref=got_s.at[slot * n_ctx + me],
                        send_sem=sem_s.at[0], recv_sem=sem_a.at[slot],
                        device_id={"ctx": owner}, device_id_type=MESH,
                    ).start()

                return 0

            lax.fori_loop(0, 2 * TILES, send_state, 0, unroll=True)

            @pl.when(lax.rem(q, 2) == lax.rem(me, 2))
            def _():
                got_s[slot * n_ctx + me] = sbuf[q * 2 * TILES + me // 2]

        return 0

    def one_quad(i, _):
        quad = quad_of(i)
        q = quad[0]
        held = dot(btr[1], weighed_block(quad, 1))
        for k in range(2, blocks):
            weighed = weighed_block(quad, k)
            sk[q, k] = held.astype(BF16)
            held = held * by_quad(dec_blk, k, q) + dot(btr[k], weighed)
        held_all[q] = held

        @pl.when(i == 1)
        def _():
            if many:
                halo_x.wait()
                halo_bc.wait()
            btr[0] = conv_bc_block(0, 0).T.astype(BF16)

        lax.fori_loop(jnp.where(i == 1, 0, i), jnp.where(i == 0, 0, i + 1), first_block, 0)
        return 0

    lax.fori_loop(0, quads, one_quad, 0)

    def all_of(sem, like, count):
        view = like.at[pl.ds(0, count)]
        pltpu.make_async_copy(view, view, sem).wait()

    def scan_part(slot):
        all_of(sem_a.at[slot], got_s, n_ctx - 1)
        base = slot * n_ctx

        def lap(d, acc):
            ret_s[base + d] = acc.astype(BF16)
            return acc * got_dec[d, slot : slot + 1, :] + got_s[base + d].astype(F32)

        lax.fori_loop(0, n_ctx, lap, jnp.zeros((PART, LANES), F32), unroll=True)
        target = (4 * slot + 2 * lax.rem(me, 2) + my_side) * TILES + my_tile

        def send_back(i, _):
            d = lax.rem(me + i, n_ctx)
            pltpu.make_async_remote_copy(
                src_ref=ret_s.at[base + d], dst_ref=inbound.at[target],
                send_sem=sem_s.at[1], recv_sem=sem_r.at[1],
                device_id={"ctx": d}, device_id_type=MESH,
            ).start()
            return 0

        lax.fori_loop(1, n_ctx, send_back, 0, unroll=True)
        inbound[target] = ret_s[base + me]

    if many:
        all_of(sem_r.at[4], got_dec, n_ctx - 1)
        scan_part(0)

    causal = iota((Q, Q), 0) >= iota((Q, Q), 1)
    for k in range(blocks):
        c_wide = conv_bc_block(k, LANES)
        c_mat = c_wide.astype(BF16)
        cwide[k * Q : (k + 1) * Q, :] = c_wide
        cmat[k * Q : (k + 1) * Q, :] = c_mat
        cb[k] = jnp.where(causal, dot(c_mat, btr[k]), 0.0).astype(BF16)
        cum = colf[k, :heads]
        ehl[k] = jnp.concatenate(two(jnp.exp2(cum)), axis=0)
        colf[k] = jnp.concatenate([cum, jnp.zeros((Q - heads, LANES), F32)], axis=0).T
        log_pre = by_pair(2 * k + 1)
        dec_pre[k] = jnp.exp2(log_pre)
        dec_one[k] = jnp.exp2(log_pre - one_on) if k else jnp.zeros_like(log_pre)
    for q in range(quads):
        sk[q, 0] = jnp.zeros((LANES, QW), BF16)
        sk[q, 1] = jnp.zeros((LANES, QW), BF16)

    for copy in load_z:
        copy.wait()
    left_bf = iota((Q, LANES), 1) < 64

    def one_block(k, _):
        rows = pl.ds(pl.multiple_of(k * Q, Q), Q)
        cb_k = cb[k]
        c_k = cmat[rows, :]
        for q in range(quads):
            out = []
            for side in range(2):
                pair = 2 * q + side
                weights = []
                for h in (2 * pair, 2 * pair + 1):
                    gap = colf[k, :, h : h + 1] + vrow[k, h : h + 1, :]
                    fade = jnp.where(causal, jnp.exp2(gap), 0.0).astype(BF16)
                    weights.append(fade * cb_k)
                x_pair = xc[q, rows, side * LANES : (side + 1) * LANES]
                zero = jnp.zeros_like(x_pair)
                both = jnp.concatenate([jnp.where(left_bf, x_pair, zero), jnp.where(left_bf, zero, x_pair)], axis=0)
                skip = jnp.where(iota((1, LANES), 1) < 64, d_skip[2 * pair], d_skip[2 * pair + 1])
                out.append(dot(jnp.concatenate(weights, axis=1), both) + skip * x_pair.astype(F32))
            fade_in = dot_t(ehl[k], sel[:, q * QW : (q + 1) * QW])
            since = jnp.concatenate([dec_one[k, 2 * q : 2 * q + 1, :], dec_one[k, 2 * q + 1 : 2 * q + 2, :]], axis=1)
            start = (sk[q, k].astype(F32) + since * fresh[q]).astype(BF16)
            inside = jnp.concatenate(out, axis=1) + fade_in * dot(c_k, start)
            gate = twice_silu_half(zq[q, rows, :].astype(F32) * 0.5)
            dec = jnp.concatenate([dec_pre[k, 2 * q : 2 * q + 1, :], dec_pre[k, 2 * q + 1 : 2 * q + 2, :]], axis=1)
            part_a[q, rows, :] = inside * gate
            part_b[q, rows, :] = fade_in * dec * gate
        return 0

    lax.fori_loop(0, split, one_block, 0)

    if many:
        scan_part(1)

    lax.fori_loop(split, blocks, one_block, 0)

    for c, end in enumerate(ends):
        spot = end - me * rows_all
        mine = jnp.where((spot >= 0) & (spot < rows_all), 1.0, 0.0)
        spot = jnp.minimum(jnp.maximum(spot, 0), rows_all - 1)
        end_c[c : c + 1, :] = cwide[pl.ds(spot, 1), :]
        for q in range(quads):
            end_a[c : c + 1, q * QW : (q + 1) * QW] = part_a[q, pl.ds(spot, 1), :] * mine
            end_b[c : c + 1, q * QW : (q + 1) * QW] = part_b[q, pl.ds(spot, 1), :] * mine

    if many:
        all_of(sem_r.at[1], inbound, 2 * n_ctx - 2)
    else:
        inbound[...] = jnp.zeros_like(inbound)
    for p in range(pairs):
        sin[:, p * LANES : (p + 1) * LANES] = inbound[p * TILES : (p + 1) * TILES].reshape(LANES, LANES)

    last = end_a[...] + end_b[...] * dot(end_c[...].astype(BF16), sin[...])
    width = heads * 64
    inv = lax.rsqrt(jnp.sum(last * last, axis=1, keepdims=True) * (1.0 / width) + 1e-05)
    rounded = (last * inv * gain[...].reshape(1, width)).astype(BF16).astype(F32)
    score = jnp.sum(rounded * readout[...].astype(F32).reshape(1, width), axis=1, keepdims=True)
    diag = iota((TABLE, LANES), 0) == iota((TABLE, LANES), 1)
    score_row = jnp.sum(jnp.where(diag, score, 0.0), axis=0, keepdims=True)
    if many:
        sc_mine[0] = score_row

        def to_head(i, _):
            pltpu.make_async_remote_copy(
                src_ref=sc_mine.at[0], dst_ref=got_h.at[me_head],
                send_sem=sem_s.at[2], recv_sem=sem_r.at[2],
                device_id={"head": lax.rem(me_head + i, n_head)}, device_id_type=MESH,
            ).start()
            return 0

        lax.fori_loop(1, n_head, to_head, 0, unroll=True)
        got_h[me_head] = score_row

    def finish(k, _):
        rows = pl.ds(pl.multiple_of(k * Q, Q), Q)
        c_k = cmat[rows, :]
        squares = jnp.zeros((Q, LANES), F32)
        for q in range(quads):
            value = part_a[q, rows, :] + part_b[q, rows, :] * dot(c_k, sin[:, q * QW : (q + 1) * QW])
            part_a[q, rows, :] = value
            square = value * value
            squares = squares + square[:, :LANES] + square[:, LANES:]
        inv = lax.rsqrt(jnp.sum(squares, axis=1, keepdims=True) * (1.0 / width) + 1e-05)
        gain_row = gain[...].reshape(1, width)
        for q in range(quads):
            mixed = part_a[q, rows, :] * inv * gain_row[:, q * QW : (q + 1) * QW]
            stage[rows, q * QW : (q + 1) * QW] = mixed.astype(BF16)
        pltpu.make_async_copy(stage.at[rows, :], out_hbm.at[rows, :], sem_out).start()
        return 0

    lax.fori_loop(0, blocks // 2, finish, 0)
    if many:
        all_of(sem_r.at[2], got_h, n_head - 1)
        score_row = jnp.sum(got_h[...], axis=0)
        sc_ctx[0] = score_row

        def to_ctx(i, _):
            pltpu.make_async_remote_copy(
                src_ref=sc_ctx.at[0], dst_ref=got_c.at[me],
                send_sem=sem_s.at[3], recv_sem=sem_r.at[3],
                device_id={"ctx": lax.rem(me + i, n_ctx)}, device_id_type=MESH,
            ).start()
            return 0

        lax.fori_loop(1, n_ctx, to_ctx, 0, unroll=True)
        got_c[me] = score_row
    lax.fori_loop(blocks // 2, blocks, finish, 0)
    if many:
        all_of(sem_s.at[0], got_s, 2 * n_ctx - 2)
        all_of(sem_s.at[1], ret_s, 2 * n_ctx - 2)
        all_of(sem_s.at[2], got_h, n_head - 1)
        all_of(sem_s.at[3], got_c, n_ctx - 1)
        all_of(sem_s.at[4], got_dec, n_ctx - 1)
        all_of(sem_r.at[3], got_c, n_ctx - 1)
        score_row = jnp.sum(got_c[...], axis=0)
    score_ref[...] = score_row[0, : score_ref.shape[0]]
    pltpu.make_async_copy(stage, out_hbm, sem_out).wait()


def local(n_ctx, n_head, x_in, gate_z, bc_in, dt_raw, conv_x, conv_bc, dt_bias, a_log, d_skip, norm_gain, readout, lengths):
    rows, width = x_in.shape
    heads = dt_raw.shape[1]
    blocks, quads, pairs = rows // Q, width // QW, heads // 2
    vmem = pl.BlockSpec(memory_space=pltpu.VMEM)
    anywhere = pl.BlockSpec(memory_space=pl.ANY)
    hbm = pl.BlockSpec(memory_space=pltpu.HBM)
    dma = pltpu.SemaphoreType.DMA
    scratch = [
        pltpu.SMEM(lengths.shape, I32),
        pltpu.SMEM(dt_bias.shape, F32),
        pltpu.SMEM(a_log.shape, F32),
        pltpu.SMEM(d_skip.shape, F32),
        pltpu.VMEM((heads, rows), F32),
        pltpu.VMEM(conv_x.shape, F32),
        pltpu.VMEM(conv_bc.shape, F32),
        pltpu.VMEM(norm_gain.shape, F32),
        pltpu.VMEM(readout.shape, BF16),
        pltpu.VMEM((quads, rows, QW), BF16),
        pltpu.VMEM((rows, 256), BF16),
        pltpu.VMEM((quads, rows, QW), BF16),
        pltpu.VMEM((HALO, width), BF16),
        pltpu.VMEM((HALO, 256), BF16),
        pltpu.VMEM((rows, LANES), F32),
        pltpu.VMEM((rows, LANES), F32),
        pltpu.VMEM((rows, LANES), F32),
        pltpu.VMEM((12, Q + 8, LANES), F32),
        pltpu.VMEM((blocks, Q, Q), F32),
        pltpu.VMEM((blocks, heads, LANES), F32),
        pltpu.VMEM((blocks, 2 * heads, LANES), BF16),
        pltpu.VMEM((blocks, 2 * heads, LANES), BF16),
        pltpu.VMEM((2 * blocks + 1, heads, LANES), F32),
        pltpu.VMEM((blocks, pairs, LANES), F32),
        pltpu.VMEM((blocks, pairs, LANES), F32),
        pltpu.VMEM((2 * heads, width), BF16),
        pltpu.VMEM((quads, rows, QW), BF16),
        pltpu.VMEM((rows, LANES), BF16),
        pltpu.VMEM((rows, LANES), F32),
        pltpu.VMEM((blocks, LANES, Q), BF16),
        pltpu.VMEM((blocks, Q, Q), BF16),
        pltpu.VMEM((quads, blocks, LANES, QW), BF16),
        pltpu.VMEM((quads, LANES, QW), F32),
        pltpu.VMEM((quads, LANES, QW), F32),
        pltpu.VMEM((blocks + 1, pairs, LANES), F32),
        pltpu.VMEM((pairs * LANES // PART, PART, LANES), BF16),
        pltpu.VMEM((quads, rows, QW), F32),
        pltpu.VMEM((quads, rows, QW), F32),
        pltpu.VMEM((rows, width), BF16),
        pltpu.VMEM((LANES, width), BF16),
        pltpu.VMEM((TABLE, width), F32),
        pltpu.VMEM((TABLE, width), F32),
        pltpu.VMEM((TABLE, LANES), F32),
        pltpu.VMEM((4, 2, LANES), F32),
        pltpu.VMEM((n_ctx, 2, LANES), F32),
        pltpu.VMEM((2 * n_ctx, PART, LANES), BF16),
        pltpu.VMEM((2 * n_ctx, PART, LANES), BF16),
        pltpu.VMEM((pairs * LANES // PART, PART, LANES), BF16),
        pltpu.VMEM((1, 1, LANES), F32),
        pltpu.VMEM((1, 1, LANES), F32),
        pltpu.VMEM((n_head, 1, LANES), F32),
        pltpu.VMEM((n_ctx, 1, LANES), F32),
        dma((9,)), dma((quads,)), dma, dma((quads,)), dma, dma((2,)), dma((2,)), dma((2,)), dma((5,)), dma((5,)),
    ]
    params = dict(vmem_limit_bytes=50 * 1024 * 1024)
    if n_ctx > 1:
        params.update(collective_id=0, has_side_effects=True)
    split = min(5, blocks)
    return pl.pallas_call(
        functools.partial(kernel, (n_ctx, n_head, rows, heads, split)),
        out_shape=(jax.ShapeDtypeStruct((rows, width), BF16), jax.ShapeDtypeStruct(lengths.shape, F32)),
        in_specs=[hbm] * 12,
        out_specs=(anywhere, vmem),
        scratch_shapes=scratch,
        compiler_params=pltpu.CompilerParams(**params),
    )(
        *(
            pltpu.with_memory_space_constraint(array, pltpu.HBM)
            for array in (
                lengths, dt_bias, a_log, d_skip,
                dt_raw.T, conv_x, conv_bc, norm_gain, readout,
                x_in, gate_z, bc_in.reshape(rows, bc_in.shape[2]),
            )
        )
    )


def solution(mesh):
    in_specs = (
        P("ctx", "head"),
        P("ctx", "head"),
        P("ctx", "head", None),
        P("ctx", "head"),
        P(None, "head"),
        P(None, "head", None),
        P("head"),
        P("head"),
        P("head"),
        P("head"),
        P("head"),
        P(),
    )
    out_specs = (P("ctx", "head"), P())
    step = functools.partial(local, mesh.shape["ctx"], mesh.shape["head"])
    return jax.shard_map(step, mesh=mesh, in_specs=in_specs, out_specs=out_specs, check_vma=False)
```

```python
import functools

import jax
import jax.numpy as jnp
from jax import lax
from jax.experimental import pallas as pl
from jax.experimental.pallas import tpu as pltpu
from jax.sharding import PartitionSpec as P

F32, BF16, I32 = jnp.float32, jnp.bfloat16, jnp.int32
MESH = pl.DeviceIdType.MESH
LOG2E = 1.4426950408889634
Q = 128
QW = 256
HALO = 16
RESET = 200.0
LANES = 128
TABLE = 16
PART = 16
TILES = LANES // PART


def iota(shape, dim):
    return lax.broadcasted_iota(I32, shape, dim)


def dot(a, b):
    return jnp.dot(a, b, preferred_element_type=F32)


def dot_t(a, b):
    return lax.dot_general(a, b, (((0,), (0,)), ((), ())), preferred_element_type=F32)


def two(x):
    hi = x.astype(BF16)
    return hi, (x - hi.astype(F32)).astype(BF16)


def three(x):
    hi = x.astype(BF16)
    return (hi,) + two(x - hi.astype(F32))


def softplus(v):
    u = jnp.exp(-jnp.abs(v))
    small = u * (1.0 + u * (-0.5 + u * (1.0 / 3.0 - 0.25 * u)))
    return jnp.maximum(v, 0.0) + jnp.where(u < 0.01, small, jnp.log(1.0 + u))


def twice_silu_half(h):
    return h + h * jnp.tanh(h)


def half_conv(rows, before, taps, keep, buf, slot):
    outs = []
    tiles = rows.shape[1] // LANES
    x = jnp.concatenate([before.astype(F32)[HALO - 8 :], rows.astype(F32)], axis=0)
    for t in range(tiles):
        buf[2 * slot + t] = x[:, t * LANES : (t + 1) * LANES]
    for t in range(tiles):
        tap = [w[:, t * LANES : (t + 1) * LANES] for w in taps]
        late = [buf[2 * slot + t, 8 - lag : 8 - lag + Q, :] for lag in (1, 2, 3)]
        acc = late[2] * tap[3] * keep[2]
        acc = (acc + late[1] * tap[2]) * keep[1]
        acc = (acc + late[0] * tap[1]) * keep[0]
        outs.append(acc + x[8:, t * LANES : (t + 1) * LANES] * tap[0])
    return outs[0] if tiles == 1 else jnp.concatenate(outs, axis=1)


def kernel(
    dims,
    lengths_hbm, bias_hbm, a_log_hbm, d_skip_hbm,
    dt_hbm, conv_x_hbm, conv_bc_hbm, gain_hbm, readout_hbm, x_hbm, z_hbm, bc_hbm,
    out_hbm, score_ref,
    lengths, bias, a_log, d_skip, dt_ref, conv_x, conv_bc, gain, readout,
    xq, bcs, zq, hx, hbc, keep, keep2, keep3, buf, colf, vrow, whl, ehl, tots, dec_blk, dec_pre, sel,
    xc, cmat, cwide, btr, cb, sk, fresh, held_all, dec_one, sbuf, part_a, part_b, stage, sin, end_a, end_b, end_c,
    my_dec, got_dec, got_s, ret_s, inbound, sc_mine, sc_ctx, got_h, got_c,
    sem_small, sem_x, sem_bc, sem_z, sem_out, sem_halo_s, sem_halo_r, sem_a, sem_s, sem_r,
):
    n_ctx, n_head, rows_all, heads, split = dims
    blocks = rows_all // Q
    quads = heads * 64 // QW
    pairs = heads // 2
    many = n_ctx > 1
    me = lax.axis_index("ctx")
    me_head = lax.axis_index("head")
    my_side, my_tile = me // 16, lax.rem(me // 2, TILES)

    load_small = [
        pltpu.make_async_copy(source, target, sem_small.at[i])
        for i, (source, target) in enumerate(
            [
                (lengths_hbm, lengths), (bias_hbm, bias), (a_log_hbm, a_log), (d_skip_hbm, d_skip),
                (dt_hbm, dt_ref), (conv_x_hbm, conv_x), (conv_bc_hbm, conv_bc), (gain_hbm, gain), (readout_hbm, readout),
            ]
        )
    ]
    for copy in load_small:
        copy.start()
    load_bc = pltpu.make_async_copy(bc_hbm, bcs, sem_bc)
    load_bc.start()
    load_x = [
        pltpu.make_async_copy(x_hbm.at[:, pl.ds(q * QW, QW)], xq.at[q], sem_x.at[q])
        for q in range(quads)
    ]
    load_z = [
        pltpu.make_async_copy(z_hbm.at[:, pl.ds(q * QW, QW)], zq.at[q], sem_z.at[q])
        for q in range(quads)
    ]
    for copy in load_x + load_z:
        copy.start()

    if many:
        barrier = pltpu.get_barrier_semaphore()

        def greet_ctx(i, _):
            pl.semaphore_signal(barrier, inc=1, device_id={"ctx": lax.rem(me + i, n_ctx)}, device_id_type=MESH)
            return 0

        lax.fori_loop(1, n_ctx, greet_ctx, 0)

        def greet_head(i, _):
            pl.semaphore_signal(barrier, inc=1, device_id={"head": lax.rem(me_head + i, n_head)}, device_id_type=MESH)
            return 0

        lax.fori_loop(1, n_head, greet_head, 0)

    for copy in load_small:
        copy.wait()

    offset = jnp.int32(0)
    here = me * rows_all + (iota((TABLE, LANES), 0) - 1) * Q + iota((TABLE, LANES), 1)
    first = jnp.zeros((TABLE, LANES), F32)
    ends = []
    for c in range(lengths.shape[0]):
        first = jnp.where(here == offset, 1.0, first)
        offset = offset + lengths[c]
        ends.append(offset - 1)

    head_row = iota((heads, LANES), 0)
    bias_col = jnp.zeros((heads, LANES), F32)
    rate_col = jnp.zeros((heads, LANES), F32)
    for h in range(heads):
        bias_col = jnp.where(head_row == h, bias[h], bias_col)
        rate_col = jnp.where(head_row == h, a_log[h], rate_col)
    rate_col = jnp.exp(rate_col) * (-LOG2E)
    steps, logs = [], []
    for k in range(blocks):
        dt_vals = softplus(dt_ref[:, k * Q : (k + 1) * Q] + bias_col)
        steps.append(jnp.log(dt_vals) * LOG2E)
        logs.append(dt_vals * rate_col - RESET * first[k + 1 : k + 2])
    upper = (iota((Q, Q), 0) <= iota((Q, Q), 1)).astype(F32).astype(BF16)
    cum_all = dot(
        jnp.concatenate(three(jnp.concatenate(logs, axis=0)), axis=1),
        jnp.concatenate([upper] * 3, axis=0),
    )
    before = jnp.zeros((heads, LANES), F32)
    for k in range(blocks):
        cum = cum_all[k * heads : (k + 1) * heads]
        value = steps[k] - cum
        total = jnp.broadcast_to(cum[:, Q - 1 : Q], (heads, LANES))
        vrow[k] = value
        colf[k, :heads] = cum
        whl[k] = jnp.concatenate(two(jnp.exp2(total + value)), axis=0)
        tots[2 * k] = total
        tots[2 * k + 1] = before
        before = before + total
    tots[2 * blocks] = before
    left = iota((pairs, LANES), 1) < 64

    def by_pair(i):
        return jnp.where(left, tots[i, pl.ds(0, pairs, stride=2), :], tots[i, pl.ds(1, pairs, stride=2), :])

    one_on = by_pair(3)
    for k in range(blocks):
        dec_blk[k] = jnp.exp2(by_pair(2 * k))
    dec_one[blocks] = jnp.exp2(by_pair(2 * blocks) - one_on)

    sel_row, sel_head = iota((2 * heads, heads * 64), 0), iota((2 * heads, heads * 64), 1) // 64
    sel[...] = jnp.where((sel_row == sel_head) | (sel_row == sel_head + heads), 1.0, 0.0).astype(BF16)
    later = 1.0 - first
    shifted = []
    for lag in (1, 2):
        here_l = pltpu.roll(later, lag, 1)
        over = jnp.concatenate([here_l[:1], here_l[:-1]], axis=0)
        shifted.append(jnp.where(iota((TABLE, LANES), 1) < lag, over, here_l))
    stay2 = later * shifted[0]
    stay3 = stay2 * shifted[1]
    keep_col = jnp.concatenate([later, stay2, stay3, jnp.zeros((LANES - 3 * TABLE, LANES), F32)], axis=0).T
    for k in range(blocks):
        for j, m in enumerate((keep, keep2, keep3)):
            m[k * Q : (k + 1) * Q, :] = jnp.broadcast_to(keep_col[:, j * TABLE + k + 1 : j * TABLE + k + 2], (Q, LANES))

    load_bc.wait()
    bc_taps = [conv_bc[lag] * 0.5 for lag in range(4)]

    def conv_bc_block(k, at):
        prev = hbc[:, at : at + LANES] if k == 0 else bcs[k * Q - HALO : k * Q, at : at + LANES]
        half = half_conv(
            bcs[k * Q : (k + 1) * Q, at : at + LANES], prev,
            [tap[:, at : at + LANES] for tap in bc_taps], [m[k * Q : (k + 1) * Q, :] for m in (keep, keep2, keep3)], buf, k % 6,
        )
        return twice_silu_half(half)

    for k in range(1, blocks):
        btr[k] = conv_bc_block(k, 0).T.astype(BF16)

    nxt = lax.rem(me + 1, n_ctx)
    if many:
        pl.semaphore_wait(barrier, n_ctx - 1 + n_head - 1)
        halo_x = pltpu.make_async_remote_copy(
            src_ref=x_hbm.at[pl.ds(rows_all - HALO, HALO), :], dst_ref=hx,
            send_sem=sem_halo_s.at[0], recv_sem=sem_halo_r.at[0],
            device_id={"ctx": nxt}, device_id_type=MESH,
        )
        halo_bc = pltpu.make_async_remote_copy(
            src_ref=bc_hbm.at[pl.ds(rows_all - HALO, HALO), :], dst_ref=hbc,
            send_sem=sem_halo_s.at[1], recv_sem=sem_halo_r.at[1],
            device_id={"ctx": nxt}, device_id_type=MESH,
        )
        halo_x.start()
        halo_bc.start()
        dec_all = jnp.exp2(by_pair(2 * blocks))
        for p in range(4):
            my_dec[p] = jnp.concatenate([dec_all[p : p + 1], dec_all[p + 4 : p + 5]], axis=0)

        def send_dec(i, _):
            other = lax.rem(me + i, n_ctx)
            pltpu.make_async_remote_copy(
                src_ref=my_dec.at[2 * lax.rem(other, 2) + other // 16], dst_ref=got_dec.at[me],
                send_sem=sem_s.at[4], recv_sem=sem_r.at[4],
                device_id={"ctx": other}, device_id_type=MESH,
            ).start()
            return 0

        lax.fori_loop(1, n_ctx, send_dec, 0, unroll=True)
        got_dec[me] = my_dec[2 * lax.rem(me, 2) + my_side]
    else:
        hx[...] = jnp.zeros_like(hx)
        hbc[...] = jnp.zeros_like(hbc)

    for copy in load_x:
        copy.wait()

    def quad_of(i):
        at = pl.multiple_of(i * QW, QW)
        return i, at, [conv_x[lag : lag + 1, pl.ds(at, QW)] * 0.5 for lag in range(4)]

    def weighed_block(quad, k):
        q, at, taps = quad
        prev = hx[:, pl.ds(at, QW)] if k == 0 else xq[q, k * Q - HALO : k * Q, :]
        half = half_conv(xq[q, k * Q : (k + 1) * Q, :], prev, taps, [m[k * Q : (k + 1) * Q, :] for m in (keep, keep2, keep3)], buf, k % 6)
        act = twice_silu_half(half).astype(BF16)
        xc[q, k * Q : (k + 1) * Q, :] = act
        return act * dot_t(whl[k], sel[:, pl.ds(at, QW)]).astype(BF16)

    def by_quad(ref, k, q):
        return jnp.concatenate([ref[k, pl.ds(2 * q, 1), :], ref[k, pl.ds(2 * q + 1, 1), :]], axis=1)

    def first_block(i, _):
        quad = quad_of(i)
        q = quad[0]
        block0 = dot(btr[0], weighed_block(quad, 0))
        fresh[q] = block0
        held = held_all[q] + block0 * by_quad(dec_one, blocks, q)
        if many:
            for u in range(2 * TILES):
                side, tile = u // TILES, u % TILES
                sbuf[q * 2 * TILES + u] = held[
                    tile * PART : (tile + 1) * PART, side * LANES : (side + 1) * LANES
                ].astype(BF16)
            slot = q // 2

            def send_state(u, _):
                owner = 2 * u + lax.rem(q, 2)

                @pl.when(owner != me)
                def _():
                    pltpu.make_async_remote_copy(
                        src_ref=sbuf.at[q * 2 * TILES + u], dst_ref=got_s.at[slot * n_ctx + me],
                        send_sem=sem_s.at[0], recv_sem=sem_a.at[slot],
                        device_id={"ctx": owner}, device_id_type=MESH,
                    ).start()

                return 0

            lax.fori_loop(0, 2 * TILES, send_state, 0, unroll=True)

            @pl.when(lax.rem(q, 2) == lax.rem(me, 2))
            def _():
                got_s[slot * n_ctx + me] = sbuf[q * 2 * TILES + me // 2]

        return 0

    def one_quad(i, _):
        quad = quad_of(i)
        q = quad[0]
        held = dot(btr[1], weighed_block(quad, 1))
        for k in range(2, blocks):
            weighed = weighed_block(quad, k)
            sk[q, k] = held.astype(BF16)
            held = held * by_quad(dec_blk, k, q) + dot(btr[k], weighed)
        held_all[q] = held

        @pl.when(i == 1)
        def _():
            if many:
                halo_x.wait()
                halo_bc.wait()
            btr[0] = conv_bc_block(0, 0).T.astype(BF16)

        lax.fori_loop(jnp.where(i == 1, 0, i), jnp.where(i == 0, 0, i + 1), first_block, 0)
        return 0

    lax.fori_loop(0, quads, one_quad, 0)

    def all_of(sem, like, count):
        view = like.at[pl.ds(0, count)]
        pltpu.make_async_copy(view, view, sem).wait()

    def scan_part(slot):
        all_of(sem_a.at[slot], got_s, n_ctx - 1)
        base = slot * n_ctx

        def lap(d, acc):
            ret_s[base + d] = acc.astype(BF16)
            return acc * got_dec[d, slot : slot + 1, :] + got_s[base + d].astype(F32)

        lax.fori_loop(0, n_ctx, lap, jnp.zeros((PART, LANES), F32), unroll=True)
        target = (4 * slot + 2 * lax.rem(me, 2) + my_side) * TILES + my_tile

        def send_back(i, _):
            d = lax.rem(me + i, n_ctx)
            pltpu.make_async_remote_copy(
                src_ref=ret_s.at[base + d], dst_ref=inbound.at[target],
                send_sem=sem_s.at[1], recv_sem=sem_r.at[1],
                device_id={"ctx": d}, device_id_type=MESH,
            ).start()
            return 0

        lax.fori_loop(1, n_ctx, send_back, 0, unroll=True)
        inbound[target] = ret_s[base + me]

    if many:
        all_of(sem_r.at[4], got_dec, n_ctx - 1)
        scan_part(0)

    causal = iota((Q, Q), 0) >= iota((Q, Q), 1)
    for k in range(blocks):
        c_wide = conv_bc_block(k, LANES)
        c_mat = c_wide.astype(BF16)
        cwide[k * Q : (k + 1) * Q, :] = c_wide
        cmat[k * Q : (k + 1) * Q, :] = c_mat
        cb[k] = jnp.where(causal, dot(c_mat, btr[k]), 0.0).astype(BF16)
        cum = colf[k, :heads]
        ehl[k] = jnp.concatenate(two(jnp.exp2(cum)), axis=0)
        colf[k] = jnp.concatenate([cum, jnp.zeros((Q - heads, LANES), F32)], axis=0).T
        log_pre = by_pair(2 * k + 1)
        dec_pre[k] = jnp.exp2(log_pre)
        dec_one[k] = jnp.exp2(log_pre - one_on) if k else jnp.zeros_like(log_pre)
    for q in range(quads):
        sk[q, 0] = jnp.zeros((LANES, QW), BF16)
        sk[q, 1] = jnp.zeros((LANES, QW), BF16)

    for copy in load_z:
        copy.wait()
    left_bf = iota((Q, LANES), 1) < 64

    def one_block(k, _):
        rows = pl.ds(pl.multiple_of(k * Q, Q), Q)
        cb_k = cb[k]
        c_k = cmat[rows, :]
        for q in range(quads):
            out = []
            for side in range(2):
                pair = 2 * q + side
                weights = []
                for h in (2 * pair, 2 * pair + 1):
                    gap = colf[k, :, h : h + 1] + vrow[k, h : h + 1, :]
                    fade = jnp.where(causal, jnp.exp2(gap), 0.0).astype(BF16)
                    weights.append(fade * cb_k)
                x_pair = xc[q, rows, side * LANES : (side + 1) * LANES]
                zero = jnp.zeros_like(x_pair)
                both = jnp.concatenate([jnp.where(left_bf, x_pair, zero), jnp.where(left_bf, zero, x_pair)], axis=0)
                skip = jnp.where(iota((1, LANES), 1) < 64, d_skip[2 * pair], d_skip[2 * pair + 1])
                out.append(dot(jnp.concatenate(weights, axis=1), both) + skip * x_pair.astype(F32))
            fade_in = dot_t(ehl[k], sel[:, q * QW : (q + 1) * QW])
            since = jnp.concatenate([dec_one[k, 2 * q : 2 * q + 1, :], dec_one[k, 2 * q + 1 : 2 * q + 2, :]], axis=1)
            start = (sk[q, k].astype(F32) + since * fresh[q]).astype(BF16)
            inside = jnp.concatenate(out, axis=1) + fade_in * dot(c_k, start)
            gate = twice_silu_half(zq[q, rows, :].astype(F32) * 0.5)
            dec = jnp.concatenate([dec_pre[k, 2 * q : 2 * q + 1, :], dec_pre[k, 2 * q + 1 : 2 * q + 2, :]], axis=1)
            part_a[q, rows, :] = inside * gate
            part_b[q, rows, :] = fade_in * dec * gate
        return 0

    lax.fori_loop(0, split, one_block, 0)

    if many:
        scan_part(1)

    lax.fori_loop(split, blocks, one_block, 0)

    for c, end in enumerate(ends):
        spot = end - me * rows_all
        mine = jnp.where((spot >= 0) & (spot < rows_all), 1.0, 0.0)
        spot = jnp.minimum(jnp.maximum(spot, 0), rows_all - 1)
        end_c[c : c + 1, :] = cwide[pl.ds(spot, 1), :]
        for q in range(quads):
            end_a[c : c + 1, q * QW : (q + 1) * QW] = part_a[q, pl.ds(spot, 1), :] * mine
            end_b[c : c + 1, q * QW : (q + 1) * QW] = part_b[q, pl.ds(spot, 1), :] * mine

    if many:
        all_of(sem_r.at[1], inbound, 2 * n_ctx - 2)
    else:
        inbound[...] = jnp.zeros_like(inbound)
    for p in range(pairs):
        sin[:, p * LANES : (p + 1) * LANES] = inbound[p * TILES : (p + 1) * TILES].reshape(LANES, LANES)

    last = end_a[...] + end_b[...] * dot(end_c[...].astype(BF16), sin[...])
    width = heads * 64
    inv = lax.rsqrt(jnp.sum(last * last, axis=1, keepdims=True) * (1.0 / width) + 1e-05)
    rounded = (last * inv * gain[...].reshape(1, width)).astype(BF16).astype(F32)
    score = jnp.sum(rounded * readout[...].astype(F32).reshape(1, width), axis=1, keepdims=True)
    diag = iota((TABLE, LANES), 0) == iota((TABLE, LANES), 1)
    score_row = jnp.sum(jnp.where(diag, score, 0.0), axis=0, keepdims=True)
    if many:
        sc_mine[0] = score_row

        def to_head(i, _):
            pltpu.make_async_remote_copy(
                src_ref=sc_mine.at[0], dst_ref=got_h.at[me_head],
                send_sem=sem_s.at[2], recv_sem=sem_r.at[2],
                device_id={"head": lax.rem(me_head + i, n_head)}, device_id_type=MESH,
            ).start()
            return 0

        lax.fori_loop(1, n_head, to_head, 0, unroll=True)
        got_h[me_head] = score_row

    def finish(k, _):
        rows = pl.ds(pl.multiple_of(k * Q, Q), Q)
        c_k = cmat[rows, :]
        squares = jnp.zeros((Q, LANES), F32)
        for q in range(quads):
            value = part_a[q, rows, :] + part_b[q, rows, :] * dot(c_k, sin[:, q * QW : (q + 1) * QW])
            part_a[q, rows, :] = value
            square = value * value
            squares = squares + square[:, :LANES] + square[:, LANES:]
        inv = lax.rsqrt(jnp.sum(squares, axis=1, keepdims=True) * (1.0 / width) + 1e-05)
        gain_row = gain[...].reshape(1, width)
        for q in range(quads):
            mixed = part_a[q, rows, :] * inv * gain_row[:, q * QW : (q + 1) * QW]
            stage[rows, q * QW : (q + 1) * QW] = mixed.astype(BF16)
        pltpu.make_async_copy(stage.at[rows, :], out_hbm.at[rows, :], sem_out).start()
        return 0

    lax.fori_loop(0, blocks // 2, finish, 0)
    if many:
        all_of(sem_r.at[2], got_h, n_head - 1)
        score_row = jnp.sum(got_h[...], axis=0)
        sc_ctx[0] = score_row

        def to_ctx(i, _):
            pltpu.make_async_remote_copy(
                src_ref=sc_ctx.at[0], dst_ref=got_c.at[me],
                send_sem=sem_s.at[3], recv_sem=sem_r.at[3],
                device_id={"ctx": lax.rem(me + i, n_ctx)}, device_id_type=MESH,
            ).start()
            return 0

        lax.fori_loop(1, n_ctx, to_ctx, 0, unroll=True)
        got_c[me] = score_row
    lax.fori_loop(blocks // 2, blocks, finish, 0)
    if many:
        all_of(sem_s.at[0], got_s, 2 * n_ctx - 2)
        all_of(sem_s.at[1], ret_s, 2 * n_ctx - 2)
        all_of(sem_s.at[2], got_h, n_head - 1)
        all_of(sem_s.at[3], got_c, n_ctx - 1)
        all_of(sem_s.at[4], got_dec, n_ctx - 1)
        all_of(sem_r.at[3], got_c, n_ctx - 1)
        score_row = jnp.sum(got_c[...], axis=0)
    score_ref[...] = score_row[0, : score_ref.shape[0]]
    pltpu.make_async_copy(stage, out_hbm, sem_out).wait()


def local(n_ctx, n_head, x_in, gate_z, bc_in, dt_raw, conv_x, conv_bc, dt_bias, a_log, d_skip, norm_gain, readout, lengths):
    rows, width = x_in.shape
    heads = dt_raw.shape[1]
    blocks, quads, pairs = rows // Q, width // QW, heads // 2
    vmem = pl.BlockSpec(memory_space=pltpu.VMEM)
    anywhere = pl.BlockSpec(memory_space=pl.ANY)
    hbm = pl.BlockSpec(memory_space=pltpu.HBM)
    dma = pltpu.SemaphoreType.DMA
    scratch = [
        pltpu.SMEM(lengths.shape, I32),
        pltpu.SMEM(dt_bias.shape, F32),
        pltpu.SMEM(a_log.shape, F32),
        pltpu.SMEM(d_skip.shape, F32),
        pltpu.VMEM((heads, rows), F32),
        pltpu.VMEM(conv_x.shape, F32),
        pltpu.VMEM(conv_bc.shape, F32),
        pltpu.VMEM(norm_gain.shape, F32),
        pltpu.VMEM(readout.shape, BF16),
        pltpu.VMEM((quads, rows, QW), BF16),
        pltpu.VMEM((rows, 256), BF16),
        pltpu.VMEM((quads, rows, QW), BF16),
        pltpu.VMEM((HALO, width), BF16),
        pltpu.VMEM((HALO, 256), BF16),
        pltpu.VMEM((rows, LANES), F32),
        pltpu.VMEM((rows, LANES), F32),
        pltpu.VMEM((rows, LANES), F32),
        pltpu.VMEM((12, Q + 8, LANES), F32),
        pltpu.VMEM((blocks, Q, Q), F32),
        pltpu.VMEM((blocks, heads, LANES), F32),
        pltpu.VMEM((blocks, 2 * heads, LANES), BF16),
        pltpu.VMEM((blocks, 2 * heads, LANES), BF16),
        pltpu.VMEM((2 * blocks + 1, heads, LANES), F32),
        pltpu.VMEM((blocks, pairs, LANES), F32),
        pltpu.VMEM((blocks, pairs, LANES), F32),
        pltpu.VMEM((2 * heads, width), BF16),
        pltpu.VMEM((quads, rows, QW), BF16),
        pltpu.VMEM((rows, LANES), BF16),
        pltpu.VMEM((rows, LANES), F32),
        pltpu.VMEM((blocks, LANES, Q), BF16),
        pltpu.VMEM((blocks, Q, Q), BF16),
        pltpu.VMEM((quads, blocks, LANES, QW), BF16),
        pltpu.VMEM((quads, LANES, QW), F32),
        pltpu.VMEM((quads, LANES, QW), F32),
        pltpu.VMEM((blocks + 1, pairs, LANES), F32),
        pltpu.VMEM((pairs * LANES // PART, PART, LANES), BF16),
        pltpu.VMEM((quads, rows, QW), F32),
        pltpu.VMEM((quads, rows, QW), F32),
        pltpu.VMEM((rows, width), BF16),
        pltpu.VMEM((LANES, width), BF16),
        pltpu.VMEM((TABLE, width), F32),
        pltpu.VMEM((TABLE, width), F32),
        pltpu.VMEM((TABLE, LANES), F32),
        pltpu.VMEM((4, 2, LANES), F32),
        pltpu.VMEM((n_ctx, 2, LANES), F32),
        pltpu.VMEM((2 * n_ctx, PART, LANES), BF16),
        pltpu.VMEM((2 * n_ctx, PART, LANES), BF16),
        pltpu.VMEM((pairs * LANES // PART, PART, LANES), BF16),
        pltpu.VMEM((1, 1, LANES), F32),
        pltpu.VMEM((1, 1, LANES), F32),
        pltpu.VMEM((n_head, 1, LANES), F32),
        pltpu.VMEM((n_ctx, 1, LANES), F32),
        dma((9,)), dma((quads,)), dma, dma((quads,)), dma, dma((2,)), dma((2,)), dma((2,)), dma((5,)), dma((5,)),
    ]
    params = dict(vmem_limit_bytes=50 * 1024 * 1024)
    if n_ctx > 1:
        params.update(collective_id=0, has_side_effects=True)
    split = min(5, blocks)
    return pl.pallas_call(
        functools.partial(kernel, (n_ctx, n_head, rows, heads, split)),
        out_shape=(jax.ShapeDtypeStruct((rows, width), BF16), jax.ShapeDtypeStruct(lengths.shape, F32)),
        in_specs=[hbm] * 12,
        out_specs=(anywhere, vmem),
        scratch_shapes=scratch,
        compiler_params=pltpu.CompilerParams(**params),
    )(
        *(
            pltpu.with_memory_space_constraint(array, pltpu.HBM)
            for array in (
                lengths, dt_bias, a_log, d_skip,
                dt_raw.T, conv_x, conv_bc, norm_gain, readout,
                x_in, gate_z, bc_in.reshape(rows, bc_in.shape[2]),
            )
        )
    )


def solution(mesh):
    in_specs = (
        P("ctx", "head"),
        P("ctx", "head"),
        P("ctx", "head", None),
        P("ctx", "head"),
        P(None, "head"),
        P(None, "head", None),
        P("head"),
        P("head"),
        P("head"),
        P("head"),
        P("head"),
        P(),
    )
    out_specs = (P("ctx", "head"), P())
    step = functools.partial(local, mesh.shape["ctx"], mesh.shape["head"])
    return jax.shard_map(step, mesh=mesh, in_specs=in_specs, out_specs=out_specs, check_vma=False)
```
